256 devices in a mesh: cores: 2 (over core), row: 16 (over y, x), vec: 8 (over z).
Axes of the slice: x: 4, y: 4, z: 8, core: 2. Of those that a mesh axis runs over, the one named last changes fastest.
Arguments:
- train_cores: float32 [8, 512, 256, 256], P('vec', 'cores', 'row'), may hold values from -0.01953125 to 0.01953125
- sketch: float32 [512, 128], P('cores'), may hold values from -6 to 6
- exit_sketch: float32 [256, 128], replicated, may hold values from -6 to 6
Outputs:
- rounded: float32 [8, 256, 256, 128], P('vec', 'cores', 'row')
- interface_bases: float32 [8, 512, 128], P('vec', 'cores')
- margins: float32 [8, 256, 1024], P('vec', 'cores')
The draws below stay inside these ranges and needn't reach their ends.
All inputs are finite; a program needn't handle non-finite values.
Results may differ from the reference program's by a relative error of at most 0.0003.
Values sent between devices are 32-bit elements; how exact they have to be, the bound alone decides.
A program may use at most 128 MiB of HBM per device.

```python
import math
import jax
import jax.numpy as jnp
from jax import lax

MODE = 256
RANK = 256
TRUNC = 128
NCORE = 2
VECS = 8


def draw_train_cores(key, part):
    block_shape = (NCORE * RANK, MODE, RANK)
    common = jax.random.normal(jax.random.fold_in(key, 21), (1,) + block_shape, jnp.float32)
    separate = jax.random.normal(jax.random.fold_in(key, 22), (VECS,) + block_shape, jnp.float32)
    common_share = 0.85
    values = math.sqrt(common_share) * common + math.sqrt(1.0 - common_share) * separate
    return (jnp.clip(values, -5.0, 5.0) / math.sqrt(RANK * MODE)).astype(jnp.float32)


def level_of(key, dims, split, smallest, high):
    loudness = 1.0
    for axis_at, parts in split:
        heights = jax.random.uniform(jax.random.fold_in(jax.random.fold_in(key, 6), axis_at), (parts,), jnp.float32, smallest / len(split), high / len(split))
        loudness = loudness * jnp.repeat(jnp.exp(heights), dims[axis_at] // parts).reshape((-1,) + (1,) * (len(dims) - 1 - axis_at))
    return loudness


def noise(stream_key, shape, spread, reach, cuts=(), kind=jnp.bfloat16):
    entries = jax.random.normal(stream_key, shape, jnp.float32) * spread
    if len(cuts) > 0:
        entries = level_of(stream_key, shape, cuts, -0.22, 0.18) * entries
    return jnp.clip(entries, min=-reach, max=reach).astype(kind)


def setup_inputs(seed: int = 0) -> dict:
    seeds = jax.random.split(jax.random.key(seed), 4)
    train_cores = draw_train_cores(jax.random.fold_in(seeds[3], 71), 0)
    sketch = noise(seeds[1], (NCORE * RANK, TRUNC), 1.0, 6.0, ((0, 2),), jnp.float32)
    exit_sketch = noise(seeds[2], (RANK, TRUNC), 1.0, 6.0, (), jnp.float32)
    return {"train_cores": train_cores, "sketch": sketch, "exit_sketch": exit_sketch}


def product(left_mat, right_mat):
    return jnp.dot(left_mat.astype(jnp.float32), right_mat.astype(jnp.float32), precision=lax.Precision.HIGHEST, preferred_element_type=jnp.float32)

def orthonormal(gram_matrix, sketch):
    powered = product(gram_matrix, product(gram_matrix, sketch))
    chol_low = jnp.linalg.cholesky(product(powered.T, powered))
    return jax.scipy.linalg.solve_triangular(chol_low, powered.T, lower=True).T

def env_step(env_in, mine, others):
    carried = jnp.einsum('qzw,qwx->qzx', env_in, others, precision=lax.Precision.HIGHEST)
    carried = carried.reshape(others.shape[0], TRUNC * MODE, TRUNC)
    return jnp.einsum('cb,qcy->qby', mine.reshape(TRUNC * MODE, TRUNC), carried, precision=lax.Precision.HIGHEST)

def reference(train_cores, sketch, exit_sketch):
    identity = jnp.eye(RANK, dtype=jnp.float32)
    pieces_all = []
    frames_all = []
    for vector in range(VECS):
        lowers = []
        grams = []
        lower_prev = identity
        for position in range(NCORE):
            block_core = train_cores[vector, position * RANK:(position + 1) * RANK].reshape(RANK, MODE * RANK)
            absorbed = product(lower_prev.T, block_core).reshape(RANK * MODE, RANK)
            gram_matrix = product(absorbed.T, absorbed)
            lower_prev = jnp.linalg.cholesky(gram_matrix)
            lowers.append(lower_prev)
            grams.append(gram_matrix)
        incoming = orthonormal(grams[-1], exit_sketch)
        pieces = [None] * NCORE
        frames = [None] * NCORE
        for position in range(NCORE - 1, -1, -1):
            block_core = train_cores[vector, position * RANK:(position + 1) * RANK].reshape(RANK * MODE, RANK)
            if position == NCORE - 1:
                right_map = incoming
            else:
                right_map = jax.scipy.linalg.solve_triangular(lowers[position], incoming, lower=True, trans=1)
            outer = identity if position == 0 else lowers[position - 1]
            mixed_core = product(outer.T, product(block_core, right_map).reshape(RANK, MODE * TRUNC))
            frame = orthonormal(product(mixed_core, mixed_core.T), sketch[position * RANK:(position + 1) * RANK])
            pieces[position] = product(frame.T, mixed_core)
            frames[position] = frame
            incoming = frame
        pieces_all.append(pieces)
        frames_all.append(frames)
    margins = []
    firsts = jnp.stack([frames_all[other][0] for other in range(VECS)])
    for vector in range(VECS):
        env_in = jnp.einsum('az,qay->qzy', frames_all[vector][0], firsts, precision=lax.Precision.HIGHEST)
        blocks = []
        for position in range(NCORE):
            others = jnp.stack([pieces_all[other][position] for other in range(VECS)])
            env_in = env_step(env_in, pieces_all[vector][position], others)
            blocks.append(env_in.transpose(1, 0, 2).reshape(TRUNC, VECS * TRUNC))
        margins.append(jnp.concatenate(blocks, axis=0))
    rounded = jnp.stack([jnp.concatenate([piece.reshape(TRUNC, MODE, TRUNC) for piece in pieces_all[vector]], axis=0) for vector in range(VECS)])
    bases_out = jnp.stack([jnp.concatenate(frames_all[vector], axis=0) for vector in range(VECS)])
    return (rounded * math.sqrt(TRUNC * MODE), bases_out * math.sqrt(RANK), jnp.stack(margins))
```

```python
import functools
import math

import jax
import jax.numpy as jnp
from jax import lax
from jax.experimental import pallas as pl
from jax.experimental.pallas import tpu as pltpu
from jax.sharding import PartitionSpec as P

MESH = pl.DeviceIdType.MESH
F32 = jnp.float32
BF16 = jnp.bfloat16
HIGHEST = lax.Precision.HIGHEST
PANEL = 16


def dot(a, b):
    return jnp.dot(a, b, preferred_element_type=F32)


def dot_nt(a, b):
    return lax.dot_general(a, b, (((1,), (1,)), ((), ())), preferred_element_type=F32)


def dot_tn(a, b):
    return lax.dot_general(a, b, (((0,), (0,)), ((), ())), preferred_element_type=F32)


def fdot(a, b):
    return jnp.dot(a, b, precision=HIGHEST, preferred_element_type=F32)


def fdot_nt(a, b):
    return lax.dot_general(
        a, b, (((1,), (1,)), ((), ())), precision=HIGHEST, preferred_element_type=F32
    )


def fdot_tn(a, b):
    return lax.dot_general(
        a, b, (((0,), (0,)), ((), ())), precision=HIGHEST, preferred_element_type=F32
    )


def split(x):
    hi = x.astype(BF16)
    lo = (x - hi.astype(F32)).astype(BF16)
    return hi, lo


def eliminate(xs, n, nb):
    lane = lax.broadcasted_iota(jnp.int32, (nb, n), 1)
    sub = lax.broadcasted_iota(jnp.int32, (nb, n), 0)

    def panel(t, carry):
        j0 = pl.multiple_of(t * nb, nb)
        v = xs[pl.ds(j0, nb), :]
        rolled = pltpu.roll(v, lax.rem(n - j0, n), 1)
        cols = [jnp.broadcast_to(rolled[:, k : k + 1], (nb, n)) for k in range(nb)]
        inv = jnp.zeros((nb, n), F32)
        for k in range(nb):
            rp = 1.0 / jnp.broadcast_to(cols[k][k : k + 1, :], (nb, n))
            inv = jnp.where(sub == k, rp, inv)
            f = jnp.where(sub > k, cols[k] * rp, 0.0)
            for m in range(k + 1, nb):
                cols[m] = cols[m] - f * cols[m][k : k + 1, :]
            pivot_row = v[k : k + 1, :]
            pivot_row = jnp.where(lane[:1] == j0 + k, 2.0 * pivot_row, pivot_row)
            v = v - f * pivot_row
        below = jnp.where(lane >= j0 + nb, v, 0.0)
        scaled = jnp.where(lane == j0 + sub, 2.0 * v, v) * inv
        xs[...] = xs[...] - fdot_tn(below, scaled)
        xs[pl.ds(j0, nb), :] = v
        return carry

    lax.fori_loop(0, n // nb, panel, 0)


def factors(xs, n):
    x = xs[...]
    rows = lax.broadcasted_iota(jnp.int32, (n, n), 0)
    lanes = lax.broadcasted_iota(jnp.int32, (n, n), 1)
    diag = jnp.where(rows == lanes, x, 0.0)
    by_row = 1.0 / jnp.sqrt(jnp.sum(diag, axis=1, keepdims=True))
    by_lane = 1.0 / jnp.sum(diag, axis=0, keepdims=True)
    lower = jnp.where(rows > lanes, x * by_lane, jnp.where(rows == lanes, 1.0, 0.0))
    upper = jnp.where(rows <= lanes, x, 0.0)
    return lower * by_row, upper * by_row


def kernel(
    sizes,
    g_hbm, w_ref, xw_ref,
    rounded_ref, bases_ref, margins_ref,
    stage, ghi, glo, gthi, gtlo, part, rs, full, lower_ref, zt_ref, xs, xcat, nw,
    ring, epart, ers, ered, xrecv, efull, ein,
    load_sem, rs_send, rs_recv, ag_send, ag_recv, pair_send, pair_recv,
    ring_send, ring_recv, ers_send, ers_recv, x_send, x_recv, eag_send, eag_recv,
):
    rank, kept, modes, rows_n, vecs = sizes
    half = vecs // 2
    mh = modes // 2
    ch = rank // rows_n
    ech = kept // rows_n
    blocks = vecs + 2 * (half - 1)
    core = lax.axis_index("cores")
    row = lax.axis_index("row")
    vec = lax.axis_index("vec")
    other = 1 - core

    pieces = load_sem.shape[0]
    prow = rank * modes // pieces
    loads = [
        pltpu.make_async_copy(
            g_hbm.at[pl.ds(t * prow, prow), pl.ds(h * 128, 128)],
            stage.at[h, pl.ds(t * prow, prow)],
            load_sem.at[t, h],
        )
        for t in range(pieces)
        for h in range(rank // 128)
    ]
    for load in loads:
        load.start()

    barrier = pltpu.get_barrier_semaphore()

    def greet(d, carry):
        there = lax.rem(row + d, rows_n)
        pl.semaphore_signal(barrier, inc=1, device_id=(core, there, vec), device_id_type=MESH)
        pl.semaphore_signal(barrier, inc=1, device_id=(other, there, vec), device_id_type=MESH)
        return carry

    lax.fori_loop(1, rows_n, greet, 0)
    pl.semaphore_signal(barrier, inc=1, device_id=(other, row, vec), device_id_type=MESH)
    away = sorted({d % vecs for d in range(-(half - 1), half)} | {1, vecs - 1})
    away = [d for d in away if d != 0]
    for d in away:
        pl.semaphore_signal(
            barrier, inc=1, device_id=(core, row, lax.rem(vec + d, vecs)), device_id_type=MESH
        )

    def meet():
        pl.semaphore_wait(barrier, 2 * (rows_n - 1) + 1 + len(away))

    def remote(src, dst, send, recv, to):
        return pltpu.make_async_remote_copy(
            src_ref=src, dst_ref=dst, send_sem=send, recv_sem=recv,
            device_id=to, device_id_type=MESH,
        )

    def pair_copy(src, dst, which):
        return remote(src, dst, pair_send.at[which], pair_recv.at[which], (other, row, vec))

    def scatter(which, to_core, first):
        def send(d, carry):
            there = lax.rem(row + d, rows_n)
            remote(
                part.at[pl.ds(there * ch, ch)], rs.at[which, d],
                rs_send.at[which], rs_recv.at[which], (to_core, there, vec),
            ).start()
            return carry

        lax.fori_loop(first, rows_n, send, 0)

    def scatter_sent(which, first):
        count = (rows_n - first) * ch
        remote(
            part.at[pl.ds(0, count)], part.at[pl.ds(0, count)],
            rs_send.at[which], rs_recv.at[which], (other, row, vec),
        ).wait_send()

    def scatter_arrived(which, first):
        view = rs.at[which, pl.ds(first, rows_n - first)]
        remote(
            view, view, rs_send.at[which], rs_recv.at[which], (other, row, vec)
        ).wait_recv()

    def gather(which):
        mine = full.at[which, pl.ds(row * ch, ch)]

        def send(d, carry):
            there = lax.rem(row + d, rows_n)
            remote(
                mine, mine, ag_send.at[which], ag_recv.at[which], (core, there, vec)
            ).start()
            return carry

        lax.fori_loop(1, rows_n, send, 0)
        view = full.at[which, pl.ds(0, (rows_n - 1) * ch)]
        done = remote(view, view, ag_send.at[which], ag_recv.at[which], (other, row, vec))
        done.wait_recv()
        done.wait_send()

    def sum_rows(which):
        scatter(which, core, 1)
        scatter_arrived(which, 1)
        total = part[pl.ds(row * ch, ch), :]
        for d in range(1, rows_n):
            total = total + rs[which, d]
        full[which, pl.ds(row * ch, ch), :] = total
        scatter_sent(which, 1)
        gather(which)

    def by_mode(with_transposes):
        def body(i, carry):
            x = jnp.concatenate(
                [stage[h, pl.ds(i, rank, stride=modes), :] for h in range(rank // 128)], axis=1
            )
            hi, lo = split(x)
            ghi[i] = hi
            glo[i] = lo
            if with_transposes:
                hi, lo = split(x.T)
                gthi[i] = hi
                gtlo[i] = lo
            return carry

        lax.fori_loop(0, modes, body, 0)

    def left_gram(z):
        zhi, zlo = split(z)
        part[...] = jnp.zeros_like(part)

        def body(i, carry):
            x = dot(ghi[i], zhi) + dot(ghi[i], zlo) + dot(glo[i], zhi)
            hi, lo = split(x)
            both = jnp.concatenate([hi, lo], axis=1)
            swapped = jnp.concatenate([lo, hi], axis=1)
            xcat[i] = both
            part[...] += dot_nt(both, both) + dot_nt(both, swapped)
            return carry

        lax.fori_loop(0, modes, body, 0)

    def whiten(yt):
        xs[...] = fdot_nt(yt, yt)
        eliminate(xs, kept, PANEL)
        return factors(xs, kept)[0]

    def shape_cores(ft):
        fhi, flo = split(ft)
        scale = math.sqrt(kept * modes * rows_n)

        def body(i, carry):
            both = xcat[i]
            r = dot(fhi, both)
            n = r[:, :kept] + r[:, kept:] + dot(flo, both[:, :kept])
            rounded_ref[pl.ds(i, kept, stride=modes), :] = n * scale
            hi, lo = split(n)
            line = jnp.concatenate([hi, lo], axis=1)
            nw[i] = jnp.concatenate([line, line], axis=0)
            at = pl.multiple_of(lax.rem(i, mh) * kept, kept)
            ring[i // mh, 0, pl.ds(at, kept), :] = n.T
            return carry

        lax.fori_loop(0, modes, body, 0)

    def ring_copy(side, k, count):
        to = lax.rem(vec + (1 if side == 0 else vecs - 1), vecs)
        return remote(
            ring.at[side, k, pl.ds(0, count)], ring.at[side, k + 1, pl.ds(0, count)],
            ring_send.at[side, k], ring_recv.at[side, k], (core, row, to),
        )

    def round_ring(count, work):
        for k in range(half):
            for side in (0, 1):
                if k > 0:
                    ring_copy(side, k - 1, count).wait_recv()
                ring_copy(side, k, count).start()
            work(k)
        for side in (0, 1):
            ring_copy(side, half - 1, count).wait_recv()
        work(half)
        for k in range(half):
            for side in (0, 1):
                ring_copy(side, k, count).wait_send()

    def carry_modes(side, k, et):
        hi, lo = split(et)
        line = jnp.concatenate([hi, lo], axis=1)
        weights = jnp.concatenate([line, line], axis=0)

        def body(i, acc):
            at = pl.multiple_of(i * kept, kept)
            hi, lo = split(ring[side, k, pl.ds(at, kept), :])
            r = dot(jnp.concatenate([hi, lo], axis=1), weights)
            hi, lo = split(r[:, :kept] + r[:, kept:])
            return acc + dot(jnp.concatenate([hi, lo], axis=1), nw[side * mh + i])

        acc = lax.fori_loop(0, mh, body, jnp.zeros((kept, 2 * kept), F32))
        return acc[:, :kept] + acc[:, kept:]

    def margin_work(k, env):
        down = lax.rem(vec + vecs - k, vecs)
        up = lax.rem(vec + k, vecs)
        first = carry_modes(0, k, env(0, k, down))
        second = carry_modes(1, k, env(1, k, up))
        if k == 0 or k == half:
            epart[down] = first + second
        else:
            epart[down] = first
            epart[up] = second
            epart[vecs + k - 1] = first.T
            epart[vecs + half - 1 + k - 1] = second.T

    def sum_margins():
        def send(d, carry):
            there = lax.rem(row + d, rows_n)
            remote(
                epart.at[:, pl.ds(there * ech, ech), :], ers.at[d],
                ers_send, ers_recv, (core, there, vec),
            ).start()
            return carry

        lax.fori_loop(1, rows_n, send, 0)
        view = ers.at[pl.ds(1, rows_n - 1)]
        done = remote(view, view, ers_send, ers_recv, (other, row, vec))
        done.wait_recv()
        total = epart[:, pl.ds(row * ech, ech), :]
        for d in range(1, rows_n):
            total = total + ers[d]
        ered[...] = total
        done.wait_send()
        count = half - 1
        for d in range(1, half):
            remote(
                ered.at[vecs + d - 1], xrecv.at[d - 1], x_send, x_recv,
                (core, row, lax.rem(vec + vecs - d, vecs)),
            ).start()
            remote(
                ered.at[vecs + count + d - 1], xrecv.at[count + d - 1], x_send, x_recv,
                (core, row, lax.rem(vec + d, vecs)),
            ).start()
        done = remote(xrecv, xrecv, x_send, x_recv, (other, row, vec))
        done.wait_recv()
        done.wait_send()
        for d in range(1, half):
            up = lax.rem(vec + d, vecs)
            down = lax.rem(vec + vecs - d, vecs)
            ered[up] = ered[up] + xrecv[d - 1]
            ered[down] = ered[down] + xrecv[count + d - 1]
        mine = efull.at[:, pl.ds(row * ech, ech), :]
        efull[:, pl.ds(row * ech, ech), :] = ered[pl.ds(0, vecs)]

        def spread(d, carry):
            there = lax.rem(row + d, rows_n)
            remote(mine, mine, eag_send, eag_recv, (core, there, vec)).start()
            return carry

        lax.fori_loop(1, rows_n, spread, 0)
        view = efull.at[:, pl.ds(0, (rows_n - 1) * ech), :]
        done = remote(view, view, eag_send, eag_recv, (other, row, vec))
        done.wait_recv()
        done.wait_send()

    def margins_out():
        for q in range(vecs):
            margins_ref[:, q * kept : (q + 1) * kept] = efull[q].T

    bases_scale = math.sqrt(rank)

    @pl.when(core == 0)
    def front():
        part[...] = jnp.zeros_like(part)
        full[0] = jnp.zeros_like(part)
        for t in range(pieces):
            for h in range(rank // 128):
                loads[t * (rank // 128) + h].wait()
            hi, lo = split(
                jnp.concatenate(
                    [stage[h, pl.ds(t * prow, prow), :] for h in range(rank // 128)], axis=1
                )
            )
            part[...] += dot_tn(hi, hi)
            full[2] = dot_tn(hi, lo) if t == 0 else full[2] + dot_tn(hi, lo)
        cross = full[2]
        part[...] += cross + cross.T
        meet()
        scatter(0, other, 0)
        by_mode(False)
        wt = w_ref[...].T
        scatter_sent(0, 0)

        pair_copy(full.at[0], full.at[0], 0).wait_recv()
        xs[...] = full[0, :kept, :kept]
        eliminate(xs, kept, PANEL)
        kinv, kt = factors(xs, kept)
        lower_ref[:kept, :kept] = kt.T
        lower_ref[:kept, kept:] = jnp.zeros((kept, rank - kept), F32)
        left = fdot_nt(full[0, kept:, :kept], kinv)
        lower_ref[kept:, :kept] = left
        xs[...] = full[0, kept:, kept:] - fdot_nt(left, left)
        eliminate(xs, kept, PANEL)
        kinv, kt = factors(xs, kept)
        lower_ref[kept:, kept:] = kt.T
        to_pair = pair_copy(lower_ref, lower_ref, 1)
        to_pair.start()

        pair_copy(zt_ref, zt_ref, 2).wait_recv()
        left_gram(zt_ref[...].T)
        sum_rows(1)
        gram = full[1]
        yt = fdot(fdot(wt, gram), gram)
        ut = fdot(whiten(yt), yt)
        bases_ref[...] = ut.T * bases_scale
        shape_cores(ut)
        for side in (0, 1):
            ring[side, 0, pl.ds(mh * kept, kept), :] = ut[:, :kept]
            ring[side, 0, pl.ds((mh + 1) * kept, kept), :] = ut[:, kept:]

        def env(side, k, q):
            a = ring[side, k, pl.ds(mh * kept, kept), :]
            b = ring[side, k, pl.ds((mh + 1) * kept, kept), :]
            c = ring[0, 0, pl.ds(mh * kept, kept), :]
            d = ring[0, 0, pl.ds((mh + 1) * kept, kept), :]
            return fdot_nt(a, c) + fdot_nt(b, d)

        round_ring((mh + 2) * kept, lambda k: margin_work(k, env))
        sum_margins()
        onward = pair_copy(efull, ein, 3)
        onward.start()
        margins_out()
        onward.wait_send()
        to_pair.wait_send()

    @pl.when(core == 1)
    def back():
        for load in loads:
            load.wait()
        by_mode(True)
        wt = w_ref[...].T
        xwt = xw_ref[...].T
        meet()
        scatter_arrived(0, 0)
        total = rs[0, 0]
        for d in range(1, rows_n):
            total = total + rs[0, d]
        full[0, pl.ds(row * ch, ch), :] = total
        gather(0)
        to_pair = pair_copy(full.at[0], full.at[0], 0)
        to_pair.start()

        chi, clo = split(full[0])
        part[...] = jnp.zeros_like(part)

        def body(i, carry):
            h = dot(gthi[i], chi) + dot(gthi[i], clo) + dot(gtlo[i], chi)
            hi, lo = split(h)
            part[...] += dot(hi, ghi[i]) + dot(hi, glo[i]) + dot(lo, ghi[i])
            return carry

        lax.fori_loop(0, modes, body, 0)
        sum_rows(1)
        gram = full[1]
        yt = fdot(fdot(xwt, gram), gram)
        ut = fdot(whiten(yt), yt)
        left_gram(ut.T)
        sum_rows(2)

        pair_copy(lower_ref, lower_ref, 1).wait_recv()
        low = lower_ref[...]
        vt = fdot_nt(wt, low)
        pt = fdot(fdot(fdot(vt, full[2]), full[0]), full[2])
        yt = fdot(pt, low)
        kinv = whiten(yt)
        zt_ref[...] = fdot(kinv, pt)
        z_pair = pair_copy(zt_ref, zt_ref, 2)
        z_pair.start()
        ut = fdot(kinv, yt)
        bases_ref[...] = ut.T * bases_scale
        shape_cores(fdot_nt(ut, low))
        round_ring(mh * kept, lambda k: None)
        pair_copy(efull, ein, 3).wait_recv()
        for k in range(half + 1):
            margin_work(k, lambda side, k, q: ein[q])
        sum_margins()
        margins_out()
        to_pair.wait_send()
        z_pair.wait_send()


def build(mesh):
    rows_n = mesh.shape["row"]
    vecs = mesh.shape["vec"]

    def local(train_cores, sketch, exit_sketch):
        _, rank, modes, _ = train_cores.shape
        kept = sketch.shape[1]
        half = vecs // 2
        mh = modes // 2
        ch = rank // rows_n
        ech = kept // rows_n
        blocks = vecs + 2 * (half - 1)
        dma = pltpu.SemaphoreType.DMA
        vmem = pl.BlockSpec(memory_space=pltpu.VMEM)
        rounded, bases, margins = pl.pallas_call(
            functools.partial(kernel, (rank, kept, modes, rows_n, vecs)),
            out_shape=(
                jax.ShapeDtypeStruct((kept * modes, kept), F32),
                jax.ShapeDtypeStruct((rank, kept), F32),
                jax.ShapeDtypeStruct((kept, vecs * kept), F32),
            ),
            in_specs=[pl.BlockSpec(memory_space=pl.ANY), vmem, vmem],
            out_specs=(vmem, vmem, vmem),
            scratch_shapes=[
                pltpu.VMEM((rank // 128, rank * modes, 128), F32),
                pltpu.VMEM((modes, rank, rank), BF16),
                pltpu.VMEM((modes, rank, rank), BF16),
                pltpu.VMEM((modes, rank, rank), BF16),
                pltpu.VMEM((modes, rank, rank), BF16),
                pltpu.VMEM((rank, rank), F32),
                pltpu.VMEM((3, rows_n, ch, rank), F32),
                pltpu.VMEM((3, rank, rank), F32),
                pltpu.VMEM((rank, rank), F32),
                pltpu.VMEM((kept, rank), F32),
                pltpu.VMEM((kept, kept), F32),
                pltpu.VMEM((modes, rank, 2 * kept), BF16),
                pltpu.VMEM((modes, 2 * kept, 2 * kept), BF16),
                pltpu.VMEM((2, half + 1, (mh + 2) * kept, kept), F32),
                pltpu.VMEM((blocks, kept, kept), F32),
                pltpu.VMEM((rows_n, blocks, ech, kept), F32),
                pltpu.VMEM((blocks, ech, kept), F32),
                pltpu.VMEM((2 * (half - 1), ech, kept), F32),
                pltpu.VMEM((vecs, kept, kept), F32),
                pltpu.VMEM((vecs, kept, kept), F32),
                dma((8, rank // 128)),
                dma((3,)), dma((3,)), dma((3,)), dma((3,)),
                dma((4,)), dma((4,)),
                dma((2, half)), dma((2, half)),
                dma, dma, dma, dma, dma, dma,
            ],
            compiler_params=pltpu.CompilerParams(
                collective_id=0, has_side_effects=True, vmem_limit_bytes=58 * 1024 * 1024
            ),
        )(train_cores.reshape(rank * modes, rank), sketch, exit_sketch)
        return (
            rounded.reshape(1, kept, modes, kept),
            bases[None],
            margins[None],
        )

    return local


def solution(mesh):
    return jax.shard_map(
        build(mesh),
        mesh=mesh,
        in_specs=(P("vec", "cores", "row", None), P("cores", None), P()),
        out_specs=(
            P("vec", "cores", "row", None),
            P("vec", "cores", None),
            P("vec", "cores", None),
        ),
        check_vma=False,
    )
```

```python
import functools
import math

import jax
import jax.numpy as jnp
from jax import lax
from jax.experimental import pallas as pl
from jax.experimental.pallas import tpu as pltpu
from jax.sharding import PartitionSpec as P

MESH = pl.DeviceIdType.MESH
F32 = jnp.float32
BF16 = jnp.bfloat16
HIGHEST = lax.Precision.HIGHEST
PANEL = 16
GROUP = 4


def dot(a, b):
    return jnp.dot(a, b, preferred_element_type=F32)


def dot_nt(a, b):
    return lax.dot_general(a, b, (((1,), (1,)), ((), ())), preferred_element_type=F32)


def dot_tn(a, b):
    return lax.dot_general(a, b, (((0,), (0,)), ((), ())), preferred_element_type=F32)


def fdot(a, b):
    return jnp.dot(a, b, precision=HIGHEST, preferred_element_type=F32)


def fdot_nt(a, b):
    return lax.dot_general(
        a, b, (((1,), (1,)), ((), ())), precision=HIGHEST, preferred_element_type=F32
    )


def fdot_tn(a, b):
    return lax.dot_general(
        a, b, (((0,), (0,)), ((), ())), precision=HIGHEST, preferred_element_type=F32
    )


def split(x):
    hi = x.astype(BF16)
    lo = (x - hi.astype(F32)).astype(BF16)
    return hi, lo


def beside(x, count):
    n = x.shape[0] // count
    return jnp.concatenate([x[m * n : (m + 1) * n] for m in range(count)], axis=1)


def eliminate(xs, n, nb):
    lane = lax.broadcasted_iota(jnp.int32, (nb, n), 1)
    sub = lax.broadcasted_iota(jnp.int32, (nb, n), 0)

    def panel(t, carry):
        j0 = pl.multiple_of(t * nb, nb)
        v = xs[pl.ds(j0, nb), :]
        rolled = pltpu.roll(v, lax.rem(n - j0, n), 1)
        cols = [jnp.broadcast_to(rolled[:, k : k + 1], (nb, n)) for k in range(nb)]
        inv = jnp.zeros((nb, n), F32)
        for k in range(nb):
            rp = 1.0 / jnp.broadcast_to(cols[k][k : k + 1, :], (nb, n))
            inv = jnp.where(sub == k, rp, inv)
            f = jnp.where(sub > k, cols[k] * rp, 0.0)
            for m in range(k + 1, nb):
                cols[m] = cols[m] - f * cols[m][k : k + 1, :]
            pivot_row = v[k : k + 1, :]
            pivot_row = jnp.where(lane[:1] == j0 + k, 2.0 * pivot_row, pivot_row)
            v = v - f * pivot_row
        below = jnp.where(lane >= j0 + nb, v, 0.0)
        scaled = jnp.where(lane == j0 + sub, 2.0 * v, v) * inv
        xs[...] = xs[...] - fdot_tn(below, scaled)
        xs[pl.ds(j0, nb), :] = v
        return carry

    lax.fori_loop(0, n // nb, panel, 0)


def factors(xs, n):
    x = xs[...]
    rows = lax.broadcasted_iota(jnp.int32, (n, n), 0)
    lanes = lax.broadcasted_iota(jnp.int32, (n, n), 1)
    diag = jnp.where(rows == lanes, x, 0.0)
    by_row = 1.0 / jnp.sqrt(jnp.sum(diag, axis=1, keepdims=True))
    by_lane = 1.0 / jnp.sum(diag, axis=0, keepdims=True)
    lower = jnp.where(rows > lanes, x * by_lane, jnp.where(rows == lanes, 1.0, 0.0))
    upper = jnp.where(rows <= lanes, x, 0.0)
    return lower * by_row, upper * by_row


def kernel(
    sizes,
    g_hbm, w_ref, xw_ref,
    rounded_ref, bases_ref, margins_ref,
    stage, ghi, glo, gthi, gtlo, part, rs, full, lower_ref, zt_ref, xs, xcat, nw,
    ring, epart, ers, xsend, xrecv, efull, ein, rounded_buf, bases_buf, margins_buf,
    load_sem, rs_send, rs_recv, ag_send, ag_recv, pair_send, pair_recv,
    ring_send, ring_recv, ers_send, ers_recv, x_send, x_recv, eag_send, eag_recv, out_sem,
):
    rank, kept, modes, rows_n, vecs = sizes
    half = vecs // 2
    mh = modes // 2
    ch = rank // rows_n
    ech = kept // rows_n
    core = lax.axis_index("cores")
    row = lax.axis_index("row")
    vec = lax.axis_index("vec")
    other = 1 - core

    pieces = load_sem.shape[0]
    prow = rank * modes // pieces
    loads = [
        pltpu.make_async_copy(
            g_hbm.at[pl.ds(t * prow, prow), pl.ds(h * 128, 128)],
            stage.at[h, pl.ds(t * prow, prow)],
            load_sem.at[t, h],
        )
        for t in range(pieces)
        for h in range(rank // 128)
    ]
    for load in loads:
        load.start()

    barrier = pltpu.get_barrier_semaphore()

    def greet(d, carry):
        there = lax.rem(row + d, rows_n)
        pl.semaphore_signal(barrier, inc=1, device_id=(core, there, vec), device_id_type=MESH)
        pl.semaphore_signal(barrier, inc=1, device_id=(other, there, vec), device_id_type=MESH)
        return carry

    lax.fori_loop(1, rows_n, greet, 0)
    pl.semaphore_signal(barrier, inc=1, device_id=(other, row, vec), device_id_type=MESH)
    away = sorted({d % vecs for d in range(-(half - 1), half)} | {1, vecs - 1})
    away = [d for d in away if d != 0]
    for d in away:
        pl.semaphore_signal(
            barrier, inc=1, device_id=(core, row, lax.rem(vec + d, vecs)), device_id_type=MESH
        )

    def meet():
        pl.semaphore_wait(barrier, 2 * (rows_n - 1) + 1 + len(away))

    def remote(src, dst, send, recv, to):
        return pltpu.make_async_remote_copy(
            src_ref=src, dst_ref=dst, send_sem=send, recv_sem=recv,
            device_id=to, device_id_type=MESH,
        )

    def pair_copy(src, dst, which):
        return remote(src, dst, pair_send.at[which], pair_recv.at[which], (other, row, vec))

    def scatter(which, to_core, first):
        def send(d, carry):
            there = lax.rem(row + d, rows_n)
            remote(
                part.at[pl.ds(there * ch, ch)], rs.at[which, d],
                rs_send.at[which], rs_recv.at[which], (to_core, there, vec),
            ).start()
            return carry

        lax.fori_loop(first, rows_n, send, 0)

    def scatter_sent(which, first):
        count = (rows_n - first) * ch
        remote(
            part.at[pl.ds(0, count)], part.at[pl.ds(0, count)],
            rs_send.at[which], rs_recv.at[which], (other, row, vec),
        ).wait_send()

    def scatter_arrived(which, first):
        view = rs.at[which, pl.ds(first, rows_n - first)]
        remote(
            view, view, rs_send.at[which], rs_recv.at[which], (other, row, vec)
        ).wait_recv()

    def gather(which):
        mine = full.at[which, pl.ds(row * ch, ch)]

        def send(d, carry):
            there = lax.rem(row + d, rows_n)
            remote(
                mine, mine, ag_send.at[which], ag_recv.at[which], (core, there, vec)
            ).start()
            return carry

        lax.fori_loop(1, rows_n, send, 0)
        view = full.at[which, pl.ds(0, (rows_n - 1) * ch)]
        done = remote(view, view, ag_send.at[which], ag_recv.at[which], (other, row, vec))
        done.wait_recv()
        done.wait_send()

    def sum_rows(which):
        scatter(which, core, 1)
        scatter_arrived(which, 1)
        total = part[pl.ds(row * ch, ch), :]
        for d in range(1, rows_n):
            total = total + rs[which, d]
        full[which, pl.ds(row * ch, ch), :] = total
        scatter_sent(which, 1)
        gather(which)

    def by_mode(with_transposes):
        def body(i, carry):
            x = jnp.concatenate(
                [stage[h, pl.ds(i, rank, stride=modes), :] for h in range(rank // 128)], axis=1
            )
            at = pl.ds(pl.multiple_of(i * rank, rank), rank)
            ghi[at, :], glo[at, :] = split(x)
            if with_transposes:
                gthi[at, :], gtlo[at, :] = split(x.T)
            return carry

        lax.fori_loop(0, modes, body, 0)

    def left_gram(z):
        zhi, zlo = split(z)
        zboth = jnp.concatenate([zhi, zlo], axis=1)
        part[...] = jnp.zeros_like(part)

        def body(i, carry):
            at = pl.ds(pl.multiple_of(i * GROUP * rank, GROUP * rank), GROUP * rank)
            r = dot(ghi[at, :], zboth)
            x = r[:, :kept] + r[:, kept:] + dot(glo[at, :], zhi)
            hi, lo = split(x)
            both = jnp.concatenate([hi, lo], axis=1)
            xcat[at, :] = both
            swapped = jnp.concatenate([lo, hi], axis=1)
            wide = beside(both, GROUP)
            part[...] += dot_nt(wide, wide) + dot_nt(wide, beside(swapped, GROUP))
            return carry

        lax.fori_loop(0, modes // GROUP, body, 0)

    def whiten(yt):
        xs[...] = fdot_nt(yt, yt)
        eliminate(xs, kept, PANEL)
        return factors(xs, kept)[0]

    scale = math.sqrt(kept * modes * rows_n)

    def shape_cores(ft, side):
        fhi, flo = split(ft)
        group = min(GROUP, mh)

        def body(t, carry):
            for m in range(group):
                i = side * mh + t * group + m
                both = xcat[pl.ds(pl.multiple_of(i * rank, rank), rank), :]
                r = dot(fhi, both)
                n = r[:, :kept] + r[:, kept:] + dot(flo, both[:, :kept])
                rounded_buf[pl.ds(i, kept, stride=modes), :] = n * scale
                hi, lo = split(n)
                line = jnp.concatenate([hi, lo], axis=1)
                at = pl.multiple_of(i * 2 * kept, 2 * kept)
                nw[pl.ds(at, kept), :] = line
                nw[pl.ds(pl.multiple_of(at + kept, kept), kept), :] = line
                at = pl.multiple_of((t * group + m) * kept, kept)
                ring[side, 0, pl.ds(at, kept), :] = n.T
            return carry

        lax.fori_loop(0, mh // group, body, 0)

    def ring_copy(side, k, count):
        to = lax.rem(vec + (1 if side == 0 else vecs - 1), vecs)
        return remote(
            ring.at[side, k, pl.ds(0, count)], ring.at[side, k + 1, pl.ds(0, count)],
            ring_send.at[side, k], ring_recv.at[side, k], (core, row, to),
        )

    def ring_step(k, count):
        for side in (0, 1):
            if k > 0:
                ring_copy(side, k - 1, count).wait_recv()
            if k < half:
                ring_copy(side, k, count).start()

    def ring_sent(count):
        for k in range(half):
            for side in (0, 1):
                ring_copy(side, k, count).wait_send()

    def carry_modes(side, k, et):
        hi, lo = split(et)
        line = jnp.concatenate([hi, lo], axis=1)
        weights = jnp.concatenate([line, line], axis=0)
        hi, lo = split(ring[side, k, pl.ds(0, mh * kept), :])
        r = dot(jnp.concatenate([hi, lo], axis=1), weights)
        hi, lo = split(r[:, :kept] + r[:, kept:])
        wide = beside(jnp.concatenate([hi, lo], axis=1), mh)
        at = side * mh * 2 * kept
        acc = dot(wide, nw[pl.ds(at, mh * 2 * kept), :])
        return acc[:, :kept] + acc[:, kept:]

    def up_at(k):
        return vecs - 1 if k == half else k

    def down_at(k):
        return 0 if k == 0 else vecs - 1 if k == half else half - 1 + k

    def swap_copy(k, side):
        to = lax.rem(vec + (vecs - k if side == 0 else k), vecs)
        return remote(
            xsend.at[k - 1, side], xrecv.at[k - 1, side], x_send.at[k - 1], x_recv.at[k - 1],
            (core, row, to),
        )

    def margin_work(k, env):
        first = carry_modes(0, k, env(0, k))
        second = carry_modes(1, k, env(1, k))
        if k == 0 or k == half:
            epart[up_at(k)] = first + second
        else:
            epart[down_at(k)] = first
            epart[up_at(k)] = second
            xsend[k - 1, 0] = first.T
            xsend[k - 1, 1] = second.T
            for side in (0, 1):
                swap_copy(k, side).start()

    def swap_done():
        for k in range(1, half):
            view = xrecv.at[k - 1]
            done = remote(view, view, x_send.at[k - 1], x_recv.at[k - 1], (other, row, vec))
            done.wait_recv()
            done.wait_send()
            epart[up_at(k)] += xrecv[k - 1, 0]
            epart[down_at(k)] += xrecv[k - 1, 1]

    spans = ((0, vecs - 1), (vecs - 1, 1))

    def margin_scatter(g):
        first, count = spans[g]

        def send(d, carry):
            there = lax.rem(row + d, rows_n)
            remote(
                epart.at[pl.ds(first, count), pl.ds(there * ech, ech), :],
                ers.at[d, pl.ds(first, count)],
                ers_send.at[g], ers_recv.at[g], (core, there, vec),
            ).start()
            return carry

        lax.fori_loop(1, rows_n, send, 0)

    def margin_gather(g):
        first, count = spans[g]
        view = ers.at[pl.ds(1, rows_n - 1), pl.ds(first, count)]
        done = remote(view, view, ers_send.at[g], ers_recv.at[g], (other, row, vec))
        done.wait_recv()
        mine = pl.ds(pl.multiple_of(row * ech, ech), ech)
        total = epart[pl.ds(first, count), mine, :]
        for d in range(1, rows_n):
            total = total + ers[d, pl.ds(first, count)]
        efull[pl.ds(first, count), mine, :] = total
        chunk = efull.at[pl.ds(first, count), mine, :]

        def spread(d, carry):
            there = lax.rem(row + d, rows_n)
            remote(
                chunk, chunk, eag_send.at[g], eag_recv.at[g], (core, there, vec)
            ).start()
            return carry

        lax.fori_loop(1, rows_n, spread, 0)
        done.wait_send()

    def margin_gathered(g):
        first, count = spans[g]
        view = efull.at[pl.ds(first, count), pl.ds(0, (rows_n - 1) * ech), :]
        done = remote(view, view, eag_send.at[g], eag_recv.at[g], (other, row, vec))
        done.wait_recv()
        done.wait_send()

    def margin_pair(g):
        first, count = spans[g]
        span = pl.ds(first, count)
        return pair_copy(efull.at[span], ein.at[span], 3 + g)

    def margins_out(g):
        first, count = spans[g]
        for at in range(first, first + count):
            away = at if at < half else at - half + 1
            shift = half if at == vecs - 1 else at if at < half else vecs - away
            q = lax.rem(vec + shift, vecs)
            lanes = pl.ds(pl.multiple_of(q * kept, kept), kept)
            margins_buf[:, lanes] = efull[at].T

    out_copies = [
        pltpu.make_async_copy(rounded_buf, rounded_ref, out_sem.at[0]),
        pltpu.make_async_copy(bases_buf, bases_ref, out_sem.at[1]),
        pltpu.make_async_copy(margins_buf, margins_ref, out_sem.at[2]),
    ]

    bases_scale = math.sqrt(rank)

    @pl.when(core == 0)
    def front():
        part[...] = jnp.zeros_like(part)
        full[0] = jnp.zeros_like(part)
        for t in range(pieces):
            for h in range(rank // 128):
                loads[t * (rank // 128) + h].wait()
            hi, lo = split(
                jnp.concatenate(
                    [stage[h, pl.ds(t * prow, prow), :] for h in range(rank // 128)], axis=1
                )
            )
            part[...] += dot_tn(hi, hi)
            full[2] = dot_tn(hi, lo) if t == 0 else full[2] + dot_tn(hi, lo)
        cross = full[2]
        part[...] += cross + cross.T
        meet()
        scatter(0, other, 0)
        by_mode(False)
        wt = w_ref[...].T
        scatter_sent(0, 0)

        pair_copy(full.at[0], full.at[0], 0).wait_recv()
        xs[...] = full[0, :kept, :kept]
        eliminate(xs, kept, PANEL)
        kinv, kt = factors(xs, kept)
        lower_ref[:kept, :kept] = kt.T
        lower_ref[:kept, kept:] = jnp.zeros((kept, rank - kept), F32)
        left = fdot_nt(full[0, kept:, :kept], kinv)
        lower_ref[kept:, :kept] = left
        xs[...] = full[0, kept:, kept:] - fdot_nt(left, left)
        eliminate(xs, kept, PANEL)
        kinv, kt = factors(xs, kept)
        lower_ref[kept:, kept:] = kt.T
        to_pair = pair_copy(lower_ref, lower_ref, 1)
        to_pair.start()

        pair_copy(zt_ref, zt_ref, 2).wait_recv()
        left_gram(zt_ref[...].T)
        sum_rows(1)
        gram = full[1]
        yt = fdot(fdot(wt, gram), gram)
        ut = fdot(whiten(yt), yt)
        bases_buf[...] = ut.T * bases_scale
        out_copies[1].start()
        count = (mh + 2) * kept
        for side in (0, 1):
            shape_cores(ut, side)
            ring[side, 0, pl.ds(mh * kept, kept), :] = ut[:, :kept]
            ring[side, 0, pl.ds((mh + 1) * kept, kept), :] = ut[:, kept:]
            ring_copy(side, 0, count).start()
        out_copies[0].start()

        def env(side, k):
            a = ring[side, k, pl.ds(mh * kept, kept), :]
            b = ring[side, k, pl.ds((mh + 1) * kept, kept), :]
            c = ring[0, 0, pl.ds(mh * kept, kept), :]
            d = ring[0, 0, pl.ds((mh + 1) * kept, kept), :]
            return fdot_nt(a, c) + fdot_nt(b, d)

        margin_work(0, env)
        for k in range(1, half):
            ring_step(k, count)
            margin_work(k, env)
        swap_done()
        margin_scatter(0)
        margin_gather(0)
        ring_step(half, count)
        margin_work(half, env)
        margin_scatter(1)
        margin_gathered(0)
        margin_pair(0).start()
        margin_gather(1)
        margins_out(0)
        margin_gathered(1)
        margin_pair(1).start()
        margins_out(1)
        out_copies[2].start()
        ring_sent(count)
        to_pair.wait_send()
        margin_pair(0).wait_send()
        margin_pair(1).wait_send()
        for copy in out_copies:
            copy.wait()

    @pl.when(core == 1)
    def back():
        for load in loads:
            load.wait()
        by_mode(True)
        wt = w_ref[...].T
        xwt = xw_ref[...].T
        meet()
        scatter_arrived(0, 0)
        total = rs[0, 0]
        for d in range(1, rows_n):
            total = total + rs[0, d]
        full[0, pl.ds(row * ch, ch), :] = total
        gather(0)
        to_pair = pair_copy(full.at[0], full.at[0], 0)
        to_pair.start()

        chi, clo = split(full[0])
        cboth = jnp.concatenate([chi, clo], axis=1)
        part[...] = jnp.zeros_like(part)

        def body(i, carry):
            at = pl.ds(pl.multiple_of(i * GROUP * rank, GROUP * rank), GROUP * rank)
            r = dot(gthi[at, :], cboth)
            h = r[:, :rank] + r[:, rank:] + dot(gtlo[at, :], chi)
            hi, lo = split(h)
            hi = beside(hi, GROUP)
            g = ghi[at, :]
            part[...] += dot(hi, g) + dot(hi, glo[at, :]) + dot(beside(lo, GROUP), g)
            return carry

        lax.fori_loop(0, modes // GROUP, body, 0)
        sum_rows(1)
        gram = full[1]
        yt = fdot(fdot(xwt, gram), gram)
        ut = fdot(whiten(yt), yt)
        left_gram(ut.T)
        sum_rows(2)

        pair_copy(lower_ref, lower_ref, 1).wait_recv()
        low = lower_ref[...]
        vt = fdot_nt(wt, low)
        pt = fdot(fdot(fdot(vt, full[2]), full[0]), full[2])
        yt = fdot(pt, low)
        kinv = whiten(yt)
        zt_ref[...] = fdot(kinv, pt)
        z_pair = pair_copy(zt_ref, zt_ref, 2)
        z_pair.start()
        ut = fdot(kinv, yt)
        bases_buf[...] = ut.T * bases_scale
        out_copies[1].start()
        ft = fdot_nt(ut, low)
        count = mh * kept
        for side in (0, 1):
            shape_cores(ft, side)
            ring_copy(side, 0, count).start()
        out_copies[0].start()
        for k in range(1, half + 1):
            ring_step(k, count)

        def env(side, k):
            return ein[down_at(k) if side == 0 else up_at(k)]

        margin_pair(0).wait_recv()
        for k in range(1, half):
            margin_work(k, env)
        margin_work(0, env)
        swap_done()
        margin_scatter(0)
        margin_pair(1).wait_recv()
        margin_work(half, env)
        margin_scatter(1)
        margin_gather(0)
        margin_gather(1)
        margin_gathered(0)
        margins_out(0)
        margin_gathered(1)
        margins_out(1)
        out_copies[2].start()
        ring_sent(count)
        to_pair.wait_send()
        z_pair.wait_send()
        for copy in out_copies:
            copy.wait()


def deliver(*refs):
    count = (len(refs) - 1) // 2
    copies = [
        pltpu.make_async_copy(refs[i], refs[count + i], refs[-1].at[i]) for i in range(count)
    ]
    for copy in copies:
        copy.start()
    for copy in copies:
        copy.wait()


def build(mesh):
    rows_n = mesh.shape["row"]
    vecs = mesh.shape["vec"]

    def local(train_cores, sketch, exit_sketch):
        _, rank, modes, _ = train_cores.shape
        kept = sketch.shape[1]
        half = vecs // 2
        mh = modes // 2
        ch = rank // rows_n
        ech = kept // rows_n
        dma = pltpu.SemaphoreType.DMA
        vmem = pl.BlockSpec(memory_space=pltpu.VMEM)
        shapes = (
            jax.ShapeDtypeStruct((kept * modes, kept), F32),
            jax.ShapeDtypeStruct((rank, kept), F32),
            jax.ShapeDtypeStruct((kept, vecs * kept), F32),
        )
        hbm = pl.BlockSpec(memory_space=pl.ANY)
        results = pl.pallas_call(
            functools.partial(kernel, (rank, kept, modes, rows_n, vecs)),
            out_shape=shapes,
            in_specs=[hbm, vmem, vmem],
            out_specs=(hbm, hbm, hbm),
            scratch_shapes=[
                pltpu.VMEM((rank // 128, rank * modes, 128), F32),
                pltpu.VMEM((modes * rank, rank), BF16),
                pltpu.VMEM((modes * rank, rank), BF16),
                pltpu.VMEM((modes * rank, rank), BF16),
                pltpu.VMEM((modes * rank, rank), BF16),
                pltpu.VMEM((rank, rank), F32),
                pltpu.VMEM((3, rows_n, ch, rank), F32),
                pltpu.VMEM((3, rank, rank), F32),
                pltpu.VMEM((rank, rank), F32),
                pltpu.VMEM((kept, rank), F32),
                pltpu.VMEM((kept, kept), F32),
                pltpu.VMEM((modes * rank, 2 * kept), BF16),
                pltpu.VMEM((modes * 2 * kept, 2 * kept), BF16),
                pltpu.VMEM((2, half + 1, (mh + 2) * kept, kept), F32),
                pltpu.VMEM((vecs, kept, kept), F32),
                pltpu.VMEM((rows_n, vecs, ech, kept), F32),
                pltpu.VMEM((half - 1, 2, kept, kept), F32),
                pltpu.VMEM((half - 1, 2, kept, kept), F32),
                pltpu.VMEM((vecs, kept, kept), F32),
                pltpu.VMEM((vecs, kept, kept), F32),
                pltpu.VMEM((kept * modes, kept), F32),
                pltpu.VMEM((rank, kept), F32),
                pltpu.VMEM((kept, vecs * kept), F32),
                dma((8, rank // 128)),
                dma((3,)), dma((3,)), dma((3,)), dma((3,)),
                dma((5,)), dma((5,)),
                dma((2, half)), dma((2, half)),
                dma((2,)), dma((2,)), dma((half - 1,)), dma((half - 1,)), dma((2,)), dma((2,)),
                dma((3,)),
            ],
            compiler_params=pltpu.CompilerParams(
                collective_id=0, has_side_effects=True, vmem_limit_bytes=58 * 1024 * 1024
            ),
        )(train_cores.reshape(rank * modes, rank), sketch, exit_sketch)
        rounded, bases, margins = pl.pallas_call(
            deliver,
            out_shape=shapes,
            in_specs=[hbm] * 3,
            out_specs=(hbm, hbm, hbm),
            scratch_shapes=[dma((3,))],
        )(*results)
        return (
            rounded.reshape(1, kept, modes, kept),
            bases[None],
            margins[None],
        )

    return local


def solution(mesh):
    return jax.shard_map(
        build(mesh),
        mesh=mesh,
        in_specs=(P("vec", "cores", "row", None), P("cores", None), P()),
        out_specs=(
            P("vec", "cores", "row", None),
            P("vec", "cores", None),
            P("vec", "cores", None),
        ),
        check_vma=False,
    )
```

```python
import functools
import math

import jax
import jax.numpy as jnp
from jax import lax
from jax.experimental import pallas as pl
from jax.experimental.pallas import tpu as pltpu
from jax.sharding import PartitionSpec as P

MESH = pl.DeviceIdType.MESH
F32 = jnp.float32
BF16 = jnp.bfloat16
HIGHEST = lax.Precision.HIGHEST
PANEL = 16
GROUP = 4


def dot(a, b):
    return jnp.dot(a, b, preferred_element_type=F32)


def dot_nt(a, b):
    return lax.dot_general(a, b, (((1,), (1,)), ((), ())), preferred_element_type=F32)


def dot_tn(a, b):
    return lax.dot_general(a, b, (((0,), (0,)), ((), ())), preferred_element_type=F32)


def fdot(a, b):
    return jnp.dot(a, b, precision=HIGHEST, preferred_element_type=F32)


def fdot_nt(a, b):
    return lax.dot_general(
        a, b, (((1,), (1,)), ((), ())), precision=HIGHEST, preferred_element_type=F32
    )


def fdot_tn(a, b):
    return lax.dot_general(
        a, b, (((0,), (0,)), ((), ())), precision=HIGHEST, preferred_element_type=F32
    )


def split(x):
    hi = x.astype(BF16)
    lo = (x - hi.astype(F32)).astype(BF16)
    return hi, lo


def beside(x, count):
    n = x.shape[0] // count
    return jnp.concatenate([x[m * n : (m + 1) * n] for m in range(count)], axis=1)


def eliminate(xs, n, nb):
    lane = lax.broadcasted_iota(jnp.int32, (nb, n), 1)
    sub = lax.broadcasted_iota(jnp.int32, (nb, n), 0)

    def panel(t, carry):
        j0 = pl.multiple_of(t * nb, nb)
        v = xs[pl.ds(j0, nb), :]
        rolled = pltpu.roll(v, lax.rem(n - j0, n), 1)
        cols = [jnp.broadcast_to(rolled[:, k : k + 1], (nb, n)) for k in range(nb)]
        inv = jnp.zeros((nb, n), F32)
        for k in range(nb):
            rp = 1.0 / jnp.broadcast_to(cols[k][k : k + 1, :], (nb, n))
            inv = jnp.where(sub == k, rp, inv)
            f = jnp.where(sub > k, cols[k] * rp, 0.0)
            for m in range(k + 1, nb):
                cols[m] = cols[m] - f * cols[m][k : k + 1, :]
            pivot_row = v[k : k + 1, :]
            pivot_row = jnp.where(lane[:1] == j0 + k, 2.0 * pivot_row, pivot_row)
            v = v - f * pivot_row
        below = jnp.where(lane >= j0 + nb, v, 0.0)
        scaled = jnp.where(lane == j0 + sub, 2.0 * v, v) * inv
        xs[...] = xs[...] - fdot_tn(below, scaled)
        xs[pl.ds(j0, nb), :] = v
        return carry

    lax.fori_loop(0, n // nb, panel, 0)


def factors(xs, n):
    x = xs[...]
    rows = lax.broadcasted_iota(jnp.int32, (n, n), 0)
    lanes = lax.broadcasted_iota(jnp.int32, (n, n), 1)
    diag = jnp.where(rows == lanes, x, 0.0)
    by_row = 1.0 / jnp.sqrt(jnp.sum(diag, axis=1, keepdims=True))
    by_lane = 1.0 / jnp.sum(diag, axis=0, keepdims=True)
    lower = jnp.where(rows > lanes, x * by_lane, jnp.where(rows == lanes, 1.0, 0.0))
    upper = jnp.where(rows <= lanes, x, 0.0)
    return lower * by_row, upper * by_row


def kernel(
    sizes,
    g_hbm, w_ref, xw_ref,
    rounded_ref, bases_ref, margins_ref,
    stage, ghi, glo, gthi, gtlo, part, rs, full, lower_ref, zt_ref, xs, xcat, nw,
    ring, epart, ers, xsend, xrecv, efull, ein, rounded_buf, bases_buf, margins_buf,
    load_sem, rs_send, rs_recv, ag_send, ag_recv, pair_send, pair_recv,
    ring_send, ring_recv, ers_send, ers_recv, x_send, x_recv, eag_send, eag_recv, out_sem,
    gring, zall, mthi, mtlo, gring_send, gring_recv, z_send, z_recv,
):
    rank, kept, modes, rows_n, vecs = sizes
    half = vecs // 2
    mh = modes // 2
    ch = rank // rows_n
    ech = kept // rows_n
    early = mh // 2
    sent = mh - early
    core = lax.axis_index("cores")
    row = lax.axis_index("row")
    vec = lax.axis_index("vec")
    other = 1 - core

    side_n = math.isqrt(rows_n)
    if side_n * side_n == rows_n and side_n > 2:
        offsets = [(a, b) for a in range(side_n) for b in range(side_n) if a or b]
        offsets.sort(key=lambda o: -sum(min(v, side_n - v) for v in o))
        peers = [
            lax.rem(row // side_n + a, side_n) * side_n + lax.rem(row % side_n + b, side_n)
            for a, b in offsets
        ]
    else:
        peers = [lax.rem(row + d, rows_n) for d in range(1, rows_n)]

    pieces = load_sem.shape[0]
    prow = rank * modes // pieces
    loads = [
        pltpu.make_async_copy(
            g_hbm.at[pl.ds(t * prow, prow), pl.ds(h * 128, 128)],
            stage.at[h, pl.ds(t * prow, prow)],
            load_sem.at[t, h],
        )
        for t in range(pieces)
        for h in range(rank // 128)
    ]
    for load in loads:
        load.start()

    barrier = pltpu.get_barrier_semaphore()

    def greet(d, carry):
        there = lax.rem(row + d, rows_n)
        pl.semaphore_signal(barrier, inc=1, device_id=(core, there, vec), device_id_type=MESH)
        pl.semaphore_signal(barrier, inc=1, device_id=(other, there, vec), device_id_type=MESH)
        return carry

    lax.fori_loop(1, rows_n, greet, 0)
    pl.semaphore_signal(barrier, inc=1, device_id=(other, row, vec), device_id_type=MESH)
    for d in range(1, vecs):
        pl.semaphore_signal(
            barrier, inc=1, device_id=(core, row, lax.rem(vec + d, vecs)), device_id_type=MESH
        )

    def meet():
        pl.semaphore_wait(barrier, 2 * (rows_n - 1) + 1 + vecs - 1)

    def remote(src, dst, send, recv, to):
        return pltpu.make_async_remote_copy(
            src_ref=src, dst_ref=dst, send_sem=send, recv_sem=recv,
            device_id=to, device_id_type=MESH,
        )

    def pair_copy(src, dst, which):
        return remote(src, dst, pair_send.at[which], pair_recv.at[which], (other, row, vec))

    def scatter(which, to_core, first):
        slots = [(d + 1, there) for d, there in enumerate(peers)]
        if first == 0:
            slots.append((0, row))
        for d, there in slots:
            remote(
                part.at[pl.ds(there * ch, ch)], rs.at[which, d],
                rs_send.at[which], rs_recv.at[which], (to_core, there, vec),
            ).start()

    def scatter_sent(which, first):
        count = (rows_n - first) * ch
        remote(
            part.at[pl.ds(0, count)], part.at[pl.ds(0, count)],
            rs_send.at[which], rs_recv.at[which], (other, row, vec),
        ).wait_send()

    def scatter_arrived(which, first):
        view = rs.at[which, pl.ds(first, rows_n - first)]
        remote(
            view, view, rs_send.at[which], rs_recv.at[which], (other, row, vec)
        ).wait_recv()

    def gather(which):
        mine = full.at[which, pl.ds(row * ch, ch)]

        for there in peers:
            remote(
                mine, mine, ag_send.at[which], ag_recv.at[which], (core, there, vec)
            ).start()
        view = full.at[which, pl.ds(0, (rows_n - 1) * ch)]
        done = remote(view, view, ag_send.at[which], ag_recv.at[which], (other, row, vec))
        done.wait_recv()
        done.wait_send()

    def sum_rows(which):
        scatter(which, core, 1)
        scatter_arrived(which, 1)
        total = part[pl.ds(row * ch, ch), :]
        for d in range(1, rows_n):
            total = total + rs[which, d]
        full[which, pl.ds(row * ch, ch), :] = total
        scatter_sent(which, 1)
        gather(which)

    def by_mode(with_transposes):
        def body(i, carry):
            x = jnp.concatenate(
                [stage[h, pl.ds(i, rank, stride=modes), :] for h in range(rank // 128)], axis=1
            )
            at = pl.ds(pl.multiple_of(i * rank, rank), rank)
            ghi[at, :], glo[at, :] = split(x)
            if not with_transposes:
                place = lax.rem(i, mh) - sent

                @pl.when(place >= 0)
                def keep():
                    to = pl.multiple_of(lax.max(place, 0) * rank, rank)
                    gring[i // mh, 0, pl.ds(to, rank), :] = x

            if with_transposes:
                gthi[at, :], gtlo[at, :] = split(x.T)
            return carry

        lax.fori_loop(0, modes, body, 0)

    def left_gram(z):
        zhi, zlo = split(z)
        zboth = jnp.concatenate([zhi, zlo], axis=1)
        part[...] = jnp.zeros_like(part)

        def body(i, carry):
            at = pl.ds(pl.multiple_of(i * GROUP * rank, GROUP * rank), GROUP * rank)
            r = dot(ghi[at, :], zboth)
            x = r[:, :kept] + r[:, kept:] + dot(glo[at, :], zhi)
            hi, lo = split(x)
            both = jnp.concatenate([hi, lo], axis=1)
            xcat[at, :] = both
            swapped = jnp.concatenate([lo, hi], axis=1)
            wide = beside(both, GROUP)
            part[...] += dot_nt(wide, wide) + dot_nt(wide, beside(swapped, GROUP))
            return carry

        lax.fori_loop(0, modes // GROUP, body, 0)

    def whiten(yt):
        xs[...] = fdot_nt(yt, yt)
        eliminate(xs, kept, PANEL)
        return factors(xs, kept)[0]

    scale = math.sqrt(kept * modes * rows_n)

    def shape_cores(ft, side):
        fhi, flo = split(ft)
        group = min(GROUP, mh)

        def body(t, carry):
            for m in range(group):
                i = side * mh + t * group + m
                both = xcat[pl.ds(pl.multiple_of(i * rank, rank), rank), :]
                r = dot(fhi, both)
                n = r[:, :kept] + r[:, kept:] + dot(flo, both[:, :kept])
                rounded_buf[pl.ds(i, kept, stride=modes), :] = n * scale
                hi, lo = split(n)
                line = jnp.concatenate([hi, lo], axis=1)
                at = pl.multiple_of(i * 2 * kept, 2 * kept)
                nw[pl.ds(at, kept), :] = line
                nw[pl.ds(pl.multiple_of(at + kept, kept), kept), :] = line
                at = pl.multiple_of((t * group + m + 2) * kept, kept)
                ring[side, 0, pl.ds(at, kept), :] = n.T
            return carry

        lax.fori_loop(0, mh // group, body, 0)

    def ring_copies(side, k, pieces):
        to = lax.rem(vec + (1 if side == 0 else vecs - 1), vecs)
        return [
            remote(
                ring.at[side, k, pl.ds(at * kept, count * kept)],
                ring.at[side, k + 1, pl.ds(at * kept, count * kept)],
                ring_send.at[side, k, n], ring_recv.at[side, k, n], (core, row, to),
            )
            for n, (at, count) in enumerate(pieces)
        ]

    def ring_step(k, pieces):
        for n in range(len(pieces)):
            for side in (0, 1):
                ring_copies(side, k - 1, pieces)[n].wait_recv()
                if k < half:
                    ring_copies(side, k, pieces)[n].start()

    def ring_sent(pieces):
        for k in range(half):
            for side in (0, 1):
                for copy in ring_copies(side, k, pieces):
                    copy.wait_send()

    def gring_copy(side, k):
        to = lax.rem(vec + (1 if side == 0 else vecs - 1), vecs)
        return remote(
            gring.at[side, k], gring.at[side, k + 1],
            gring_send.at[side, k], gring_recv.at[side, k], (core, row, to),
        )

    def gring_step(k):
        for side in (0, 1):
            if k > 0:
                gring_copy(side, k - 1).wait_recv()
            if k < half:
                gring_copy(side, k).start()

    def z_copy(d):
        return remote(
            zt_ref, zall.at[vecs - d], z_send.at[d], z_recv.at[vecs - d],
            (core, row, lax.rem(vec + d, vecs)),
        )

    def z_arrived(d):
        remote(
            zall.at[d], zall.at[d], z_send.at[d], z_recv.at[d], (other, row, vec)
        ).wait_recv()

    def early_maps(k):
        for side in (0, 1):
            d = vecs - k if side == 0 else k
            if side == 0 or d != vecs - k:
                z_arrived(d)
            zhi, zlo = split(zall[d])
            for e in range(early):
                hi, lo = split(gring[side, k, e * rank : (e + 1) * rank, :])
                m = dot_nt(zhi, hi) + dot_nt(zhi, lo) + dot_nt(zlo, hi)
                at = slice(e * kept, (e + 1) * kept)
                mthi[side, at, :], mtlo[side, at, :] = split(m)

    def early_cores(k):
        for side in (0, 1):
            u = jnp.concatenate([ring[side, k, :kept, :], ring[side, k, kept : 2 * kept, :]], 1)
            uhi, ulo = split(u)
            m = mthi[side]
            ring[side, k, (2 + sent) * kept :, :] = (
                dot_nt(m, uhi) + dot_nt(m, ulo) + dot_nt(mtlo[side], uhi)
            )

    def carry_modes(side, k, et):
        hi, lo = split(et)
        line = jnp.concatenate([hi, lo], axis=1)
        weights = jnp.concatenate([line, line], axis=0)
        hi, lo = split(ring[side, k, 2 * kept :, :])
        r = dot(jnp.concatenate([hi, lo], axis=1), weights)
        hi, lo = split(r[:, :kept] + r[:, kept:])
        wide = beside(jnp.concatenate([hi, lo], axis=1), mh)
        at = side * mh * 2 * kept
        acc = dot(wide, nw[pl.ds(at, mh * 2 * kept), :])
        return acc[:, :kept] + acc[:, kept:]

    def up_at(k):
        return vecs - 1 if k == half else k

    def down_at(k):
        return 0 if k == 0 else vecs - 1 if k == half else half - 1 + k

    def swap_copy(k, side):
        to = lax.rem(vec + (vecs - k if side == 0 else k), vecs)
        return remote(
            xsend.at[k - 1, side], xrecv.at[k - 1, side], x_send.at[k - 1], x_recv.at[k - 1],
            (core, row, to),
        )

    def margin_work(k, env):
        first = carry_modes(0, k, env(0, k))
        second = carry_modes(1, k, env(1, k))
        if k == 0 or k == half:
            epart[up_at(k)] = first + second
        else:
            epart[down_at(k)] = first
            epart[up_at(k)] = second
            xsend[k - 1, 0] = first.T
            xsend[k - 1, 1] = second.T
            for side in (0, 1):
                swap_copy(k, side).start()

    def swap_done():
        for k in range(1, half):
            view = xrecv.at[k - 1]
            done = remote(view, view, x_send.at[k - 1], x_recv.at[k - 1], (other, row, vec))
            done.wait_recv()
            done.wait_send()
            epart[up_at(k)] += xrecv[k - 1, 0]
            epart[down_at(k)] += xrecv[k - 1, 1]

    spans = ((0, vecs - 1), (vecs - 1, 1))

    def margin_scatter(g):
        first, count = spans[g]

        for d, there in enumerate(peers, 1):
            remote(
                epart.at[pl.ds(first, count), pl.ds(there * ech, ech), :],
                ers.at[d, pl.ds(first, count)],
                ers_send.at[g], ers_recv.at[g], (core, there, vec),
            ).start()

    def margin_gather(g):
        first, count = spans[g]
        view = ers.at[pl.ds(1, rows_n - 1), pl.ds(first, count)]
        done = remote(view, view, ers_send.at[g], ers_recv.at[g], (other, row, vec))
        done.wait_recv()
        mine = pl.ds(pl.multiple_of(row * ech, ech), ech)
        total = epart[pl.ds(first, count), mine, :]
        for d in range(1, rows_n):
            total = total + ers[d, pl.ds(first, count)]
        efull[pl.ds(first, count), mine, :] = total
        chunk = efull.at[pl.ds(first, count), mine, :]

        for there in peers:
            remote(
                chunk, chunk, eag_send.at[g], eag_recv.at[g], (core, there, vec)
            ).start()
        done.wait_send()

    def margin_gathered(g):
        first, count = spans[g]
        view = efull.at[pl.ds(first, count), pl.ds(0, (rows_n - 1) * ech), :]
        done = remote(view, view, eag_send.at[g], eag_recv.at[g], (other, row, vec))
        done.wait_recv()
        done.wait_send()

    def margin_pair(g):
        first, count = spans[g]
        span = pl.ds(first, count)
        return pair_copy(efull.at[span], ein.at[span], 3 + g)

    def margins_out(g):
        first, count = spans[g]
        for at in range(first, first + count):
            away = at if at < half else at - half + 1
            shift = half if at == vecs - 1 else at if at < half else vecs - away
            q = lax.rem(vec + shift, vecs)
            lanes = pl.ds(pl.multiple_of(q * kept, kept), kept)
            margins_buf[:, lanes] = efull[at].T

    out_copies = [
        pltpu.make_async_copy(rounded_buf, rounded_ref, out_sem.at[0]),
        pltpu.make_async_copy(bases_buf, bases_ref, out_sem.at[1]),
        pltpu.make_async_copy(margins_buf, margins_ref, out_sem.at[2]),
    ]

    bases_scale = math.sqrt(rank)

    @pl.when(core == 0)
    def front():
        part[...] = jnp.zeros_like(part)
        full[0] = jnp.zeros_like(part)
        for t in range(pieces):
            for h in range(rank // 128):
                loads[t * (rank // 128) + h].wait()
            hi, lo = split(
                jnp.concatenate(
                    [stage[h, pl.ds(t * prow, prow), :] for h in range(rank // 128)], axis=1
                )
            )
            part[...] += dot_tn(hi, hi)
            full[2] = dot_tn(hi, lo) if t == 0 else full[2] + dot_tn(hi, lo)
        cross = full[2]
        part[...] += cross + cross.T
        meet()
        scatter(0, other, 0)
        by_mode(False)
        gring_step(0)
        wt = w_ref[...].T
        scatter_sent(0, 0)

        pair_copy(full.at[0], full.at[0], 0).wait_recv()
        xs[...] = full[0, :kept, :kept]
        eliminate(xs, kept, PANEL)
        kinv, kt = factors(xs, kept)
        gring_step(1)
        lower_ref[:kept, :kept] = kt.T
        lower_ref[:kept, kept:] = jnp.zeros((kept, rank - kept), F32)
        left = fdot_nt(full[0, kept:, :kept], kinv)
        lower_ref[kept:, :kept] = left
        xs[...] = full[0, kept:, kept:] - fdot_nt(left, left)
        eliminate(xs, kept, PANEL)
        kinv, kt = factors(xs, kept)
        lower_ref[kept:, kept:] = kt.T
        to_pair = pair_copy(lower_ref, lower_ref, 1)
        to_pair.start()

        for k in range(2, half):
            gring_step(k)
        pair_copy(zt_ref, zt_ref, 2).wait_recv()
        for d in range(1, vecs):
            z_copy(d).start()
        left_gram(zt_ref[...].T)
        sum_rows(1)
        gram = full[1]
        yt = fdot(fdot(wt, gram), gram)
        ut = fdot(whiten(yt), yt)
        bases_buf[...] = ut.T * bases_scale
        out_copies[1].start()
        cuts = [(0, 2), (2, sent)]
        for side in (0, 1):
            ring[side, 0, :kept, :] = ut[:, :kept]
            ring[side, 0, kept : 2 * kept, :] = ut[:, kept:]
            ring_copies(side, 0, cuts)[0].start()
        for side in (0, 1):
            shape_cores(ft=ut, side=side)
            ring_copies(side, 0, cuts)[1].start()
        out_copies[0].start()
        gring_step(half)

        def env(side, k):
            a = ring[side, k, :kept, :]
            b = ring[side, k, kept : 2 * kept, :]
            c = ring[0, 0, :kept, :]
            d = ring[0, 0, kept : 2 * kept, :]
            return fdot_nt(a, c) + fdot_nt(b, d)

        margin_work(0, env)
        for k in range(1, half):
            early_maps(k)
            ring_step(k, cuts)
            early_cores(k)
            margin_work(k, env)
        early_maps(half)
        swap_done()
        margin_scatter(0)
        margin_gather(0)
        ring_step(half, cuts)
        early_cores(half)
        margin_work(half, env)
        margin_scatter(1)
        margin_gathered(0)
        margin_pair(0).start()
        margin_gather(1)
        margins_out(0)
        margin_gathered(1)
        margin_pair(1).start()
        margins_out(1)
        out_copies[2].start()
        ring_sent(cuts)
        for d in range(1, vecs):
            z_copy(d).wait_send()
        for k in range(half):
            for side in (0, 1):
                gring_copy(side, k).wait_send()
        to_pair.wait_send()
        margin_pair(0).wait_send()
        margin_pair(1).wait_send()
        for copy in out_copies:
            copy.wait()

    @pl.when(core == 1)
    def back():
        for load in loads:
            load.wait()
        by_mode(True)
        wt = w_ref[...].T
        xwt = xw_ref[...].T
        meet()
        scatter_arrived(0, 0)
        total = rs[0, 0]
        for d in range(1, rows_n):
            total = total + rs[0, d]
        full[0, pl.ds(row * ch, ch), :] = total
        gather(0)
        to_pair = pair_copy(full.at[0], full.at[0], 0)
        to_pair.start()

        chi, clo = split(full[0])
        cboth = jnp.concatenate([chi, clo], axis=1)
        part[...] = jnp.zeros_like(part)

        def body(i, carry):
            at = pl.ds(pl.multiple_of(i * GROUP * rank, GROUP * rank), GROUP * rank)
            r = dot(gthi[at, :], cboth)
            h = r[:, :rank] + r[:, rank:] + dot(gtlo[at, :], chi)
            hi, lo = split(h)
            hi = beside(hi, GROUP)
            g = ghi[at, :]
            part[...] += dot(hi, g) + dot(hi, glo[at, :]) + dot(beside(lo, GROUP), g)
            return carry

        lax.fori_loop(0, modes // GROUP, body, 0)
        sum_rows(1)
        gram = full[1]
        yt = fdot(fdot(xwt, gram), gram)
        ut = fdot(whiten(yt), yt)
        left_gram(ut.T)
        sum_rows(2)

        pair_copy(lower_ref, lower_ref, 1).wait_recv()
        low = lower_ref[...]
        vt = fdot_nt(wt, low)
        pt = fdot(fdot(fdot(vt, full[2]), full[0]), full[2])
        yt = fdot(pt, low)
        kinv = whiten(yt)
        zt_ref[...] = fdot(kinv, pt)
        z_pair = pair_copy(zt_ref, zt_ref, 2)
        z_pair.start()
        ut = fdot(kinv, yt)
        bases_buf[...] = ut.T * bases_scale
        out_copies[1].start()
        ft = fdot_nt(ut, low)
        cuts = [(2, sent), (2 + sent, early)]
        for side in (0, 1):
            shape_cores(ft, side)
            for copy in ring_copies(side, 0, cuts):
                copy.start()
        out_copies[0].start()
        for k in range(1, half + 1):
            ring_step(k, cuts)

        def env(side, k):
            return ein[down_at(k) if side == 0 else up_at(k)]

        margin_pair(0).wait_recv()
        for k in range(1, half):
            margin_work(k, env)
        margin_work(0, env)
        swap_done()
        margin_scatter(0)
        margin_pair(1).wait_recv()
        margin_work(half, env)
        margin_scatter(1)
        margin_gather(0)
        margin_gather(1)
        margin_gathered(0)
        margins_out(0)
        margin_gathered(1)
        margins_out(1)
        out_copies[2].start()
        ring_sent(cuts)
        to_pair.wait_send()
        z_pair.wait_send()
        for copy in out_copies:
            copy.wait()


def deliver(*refs):
    sources, targets, buffers = refs[:3], refs[3:6], refs[6:9]
    into, out = refs[9:]
    spans = [
        (n, pl.ds(t * (src.shape[0] // count), src.shape[0] // count))
        for n, (src, count) in enumerate(zip(sources, (4, 1, 2)))
        for t in range(count)
    ]
    loads = [
        pltpu.make_async_copy(sources[n].at[span], buffers[n].at[span], into.at[t])
        for t, (n, span) in enumerate(spans)
    ]
    stores = [
        pltpu.make_async_copy(buffers[n].at[span], targets[n].at[span], out.at[t])
        for t, (n, span) in enumerate(spans)
    ]
    for copy in loads:
        copy.start()
    for load, store in zip(loads, stores):
        load.wait()
        store.start()
    for store in stores:
        store.wait()


def build(mesh):
    rows_n = mesh.shape["row"]
    vecs = mesh.shape["vec"]

    def local(train_cores, sketch, exit_sketch):
        _, rank, modes, _ = train_cores.shape
        kept = sketch.shape[1]
        half = vecs // 2
        mh = modes // 2
        early = mh // 2
        ch = rank // rows_n
        ech = kept // rows_n
        dma = pltpu.SemaphoreType.DMA
        vmem = pl.BlockSpec(memory_space=pltpu.VMEM)
        shapes = (
            jax.ShapeDtypeStruct((kept * modes, kept), F32),
            jax.ShapeDtypeStruct((rank, kept), F32),
            jax.ShapeDtypeStruct((kept, vecs * kept), F32),
        )
        hbm = pl.BlockSpec(memory_space=pl.ANY)
        results = pl.pallas_call(
            functools.partial(kernel, (rank, kept, modes, rows_n, vecs)),
            out_shape=shapes,
            in_specs=[hbm, vmem, vmem],
            out_specs=(hbm, hbm, hbm),
            scratch_shapes=[
                pltpu.VMEM((rank // 128, rank * modes, 128), F32),
                pltpu.VMEM((modes * rank, rank), BF16),
                pltpu.VMEM((modes * rank, rank), BF16),
                pltpu.VMEM((modes * rank, rank), BF16),
                pltpu.VMEM((modes * rank, rank), BF16),
                pltpu.VMEM((rank, rank), F32),
                pltpu.VMEM((3, rows_n, ch, rank), F32),
                pltpu.VMEM((3, rank, rank), F32),
                pltpu.VMEM((rank, rank), F32),
                pltpu.VMEM((kept, rank), F32),
                pltpu.VMEM((kept, kept), F32),
                pltpu.VMEM((modes * rank, 2 * kept), BF16),
                pltpu.VMEM((modes * 2 * kept, 2 * kept), BF16),
                pltpu.VMEM((2, half + 1, (mh + 2) * kept, kept), F32),
                pltpu.VMEM((vecs, kept, kept), F32),
                pltpu.VMEM((rows_n, vecs, ech, kept), F32),
                pltpu.VMEM((half - 1, 2, kept, kept), F32),
                pltpu.VMEM((half - 1, 2, kept, kept), F32),
                pltpu.VMEM((vecs, kept, kept), F32),
                pltpu.VMEM((vecs, kept, kept), F32),
                pltpu.VMEM((kept * modes, kept), F32),
                pltpu.VMEM((rank, kept), F32),
                pltpu.VMEM((kept, vecs * kept), F32),
                dma((8, rank // 128)),
                dma((3,)), dma((3,)), dma((3,)), dma((3,)),
                dma((5,)), dma((5,)),
                dma((2, half, 2)), dma((2, half, 2)),
                dma((2,)), dma((2,)), dma((half - 1,)), dma((half - 1,)), dma((2,)), dma((2,)),
                dma((3,)),
                pltpu.VMEM((2, half + 1, early * rank, rank), F32),
                pltpu.VMEM((vecs, kept, rank), F32),
                pltpu.VMEM((2, early * kept, rank), BF16),
                pltpu.VMEM((2, early * kept, rank), BF16),
                dma((2, half)), dma((2, half)), dma((vecs,)), dma((vecs,)),
            ],
            compiler_params=pltpu.CompilerParams(
                collective_id=0, has_side_effects=True, vmem_limit_bytes=58 * 1024 * 1024
            ),
        )(train_cores.reshape(rank * modes, rank), sketch, exit_sketch)
        rounded, bases, margins = pl.pallas_call(
            deliver,
            out_shape=shapes,
            in_specs=[hbm] * 3,
            out_specs=(hbm, hbm, hbm),
            scratch_shapes=[pltpu.VMEM(x.shape, F32) for x in shapes] + [dma((7,)), dma((7,))],
        )(*results)
        return (
            rounded.reshape(1, kept, modes, kept),
            bases[None],
            margins[None],
        )

    return local


def solution(mesh):
    return jax.shard_map(
        build(mesh),
        mesh=mesh,
        in_specs=(P("vec", "cores", "row", None), P("cores", None), P()),
        out_specs=(
            P("vec", "cores", "row", None),
            P("vec", "cores", None),
            P("vec", "cores", None),
        ),
        check_vma=False,
    )
```

```python
import functools
import math

import jax
import jax.numpy as jnp
from jax import lax
from jax.experimental import pallas as pl
from jax.experimental.pallas import tpu as pltpu
from jax.sharding import PartitionSpec as P

MESH = pl.DeviceIdType.MESH
F32 = jnp.float32
BF16 = jnp.bfloat16
HIGHEST = lax.Precision.HIGHEST
PANEL = 16
GROUP = 2
EARLY = 3


def dot(a, b):
    return jnp.dot(a, b, preferred_element_type=F32)


def dot_nt(a, b):
    return lax.dot_general(a, b, (((1,), (1,)), ((), ())), preferred_element_type=F32)


def dot_tn(a, b):
    return lax.dot_general(a, b, (((0,), (0,)), ((), ())), preferred_element_type=F32)


def fdot(a, b):
    return jnp.dot(a, b, precision=HIGHEST, preferred_element_type=F32)


def fdot_nt(a, b):
    return lax.dot_general(
        a, b, (((1,), (1,)), ((), ())), precision=HIGHEST, preferred_element_type=F32
    )


def fdot_tn(a, b):
    return lax.dot_general(
        a, b, (((0,), (0,)), ((), ())), precision=HIGHEST, preferred_element_type=F32
    )


def split(x):
    hi = x.astype(BF16)
    lo = (x - hi.astype(F32)).astype(BF16)
    return hi, lo


def beside(x, count):
    n = x.shape[0] // count
    return jnp.concatenate([x[m * n : (m + 1) * n] for m in range(count)], axis=1)


def three(x):
    a = x.astype(BF16)
    rest = x - a.astype(F32)
    b = rest.astype(BF16)
    return a, b, (rest - b.astype(F32)).astype(BF16)


def eliminate(xs, n, nb, unrolled=True):
    lane = lax.broadcasted_iota(jnp.int32, (nb, n), 1)
    sub = lax.broadcasted_iota(jnp.int32, (nb, n), 0)

    def panel(t, carry):
        if unrolled:
            j0 = t * nb
            v = xs[j0 : j0 + nb, :]
            square = v[:, j0 : j0 + nb]
        else:
            j0 = pl.multiple_of(t * nb, nb)
            v = xs[pl.ds(j0, nb), :]
            square = pltpu.roll(v, lax.rem(n - j0, n), 1)[:, :nb]
        cols = jnp.stack([jnp.broadcast_to(square[:, k : k + 1], (nb, n)) for k in range(nb)])
        inv = jnp.zeros((nb, n), F32)
        for k in range(nb):
            rp = jnp.broadcast_to(1.0 / cols[0, k : k + 1, :], (nb, n))
            inv = jnp.where(sub == k, rp, inv)
            f = jnp.where(sub > k, cols[0] * rp, 0.0)
            if k + 1 < nb:
                cols = cols[1:]
                cols = cols - f[None] * cols[:, k : k + 1, :]
            pivot_row = v[k : k + 1, :]
            pivot_row = jnp.where(lane[:1] == j0 + k, 2.0 * pivot_row, pivot_row)
            v = v - f * pivot_row
        below = jnp.where(lane >= j0 + nb, v, 0.0)
        scaled = jnp.where(lane == j0 + sub, 2.0 * v, v) * inv
        a, b, c = three(below)
        d, e, g = three(scaled)
        update = dot_tn(
            jnp.concatenate([a, a, b, a, b, c], axis=0), jnp.concatenate([d, e, d, g, e, d], axis=0)
        )
        xs[...] = xs[...] - update
        xs[pl.ds(j0, nb), :] = v
        return carry

    if unrolled:
        for t in range(n // nb):
            panel(t, 0)
    else:
        lax.fori_loop(0, n // nb, panel, 0)


def factors(xs, n):
    x = xs[...]
    rows = lax.broadcasted_iota(jnp.int32, (n, n), 0)
    lanes = lax.broadcasted_iota(jnp.int32, (n, n), 1)
    diag = jnp.where(rows == lanes, x, 0.0)
    by_row = 1.0 / jnp.sqrt(jnp.sum(diag, axis=1, keepdims=True))
    by_lane = 1.0 / jnp.sum(diag, axis=0, keepdims=True)
    lower = jnp.where(rows > lanes, x * by_lane, jnp.where(rows == lanes, 1.0, 0.0))
    upper = jnp.where(rows <= lanes, x, 0.0)
    return lower * by_row, upper * by_row


def kernel(
    sizes,
    g_hbm, w_ref, xw_ref,
    rounded_ref, bases_ref, margins_ref,
    stage, ghi, glo, gthi, gtlo, part, rs, full, lower_ref, zt_ref, xs, xcat, nw,
    ring, epart, ers, xsend, xrecv, efull, ein, rounded_buf, bases_buf, margins_buf,
    load_sem, rs_send, rs_recv, ag_send, ag_recv, pair_send, pair_recv,
    ring_send, ring_recv, ers_send, ers_recv, x_send, x_recv, eag_send, eag_recv, out_sem,
    gring, zall, mthi, mtlo, gring_send, gring_recv, z_send, z_recv,
):
    rank, kept, modes, rows_n, vecs = sizes
    half = vecs // 2
    mh = modes // 2
    ch = rank // rows_n
    ech = kept // rows_n
    early = EARLY if mh > EARLY else mh // 2
    sent = mh - early
    core = lax.axis_index("cores")
    row = lax.axis_index("row")
    vec = lax.axis_index("vec")
    other = 1 - core

    side_n = math.isqrt(rows_n)
    if side_n * side_n == rows_n and side_n > 2:
        offsets = [(a, b) for a in range(side_n) for b in range(side_n) if a or b]
        offsets.sort(key=lambda o: -sum(min(v, side_n - v) for v in o))
        peers = [
            lax.rem(row // side_n + a, side_n) * side_n + lax.rem(row % side_n + b, side_n)
            for a, b in offsets
        ]
    else:
        peers = [lax.rem(row + d, rows_n) for d in range(1, rows_n)]

    pieces = load_sem.shape[0]
    prow = rank * modes // pieces
    loads = [
        pltpu.make_async_copy(
            g_hbm.at[pl.ds(t * prow, prow), pl.ds(h * 128, 128)],
            stage.at[h, pl.ds(t * prow, prow)],
            load_sem.at[t, h],
        )
        for t in range(pieces)
        for h in range(rank // 128)
    ]
    for load in loads:
        load.start()

    barrier = pltpu.get_barrier_semaphore()

    def greet(d, carry):
        there = lax.rem(row + d, rows_n)
        pl.semaphore_signal(barrier, inc=1, device_id=(core, there, vec), device_id_type=MESH)
        pl.semaphore_signal(barrier, inc=1, device_id=(other, there, vec), device_id_type=MESH)
        return carry

    lax.fori_loop(1, rows_n, greet, 0)
    pl.semaphore_signal(barrier, inc=1, device_id=(other, row, vec), device_id_type=MESH)
    for d in range(1, vecs):
        pl.semaphore_signal(
            barrier, inc=1, device_id=(core, row, lax.rem(vec + d, vecs)), device_id_type=MESH
        )

    def meet():
        pl.semaphore_wait(barrier, 2 * (rows_n - 1) + 1 + vecs - 1)

    def remote(src, dst, send, recv, to):
        return pltpu.make_async_remote_copy(
            src_ref=src, dst_ref=dst, send_sem=send, recv_sem=recv,
            device_id=to, device_id_type=MESH,
        )

    def pair_copy(src, dst, which):
        return remote(src, dst, pair_send.at[which], pair_recv.at[which], (other, row, vec))

    def scatter(which, to_core, first):
        slots = [(d + 1, there) for d, there in enumerate(peers)]
        if first == 0:
            slots.append((0, row))
        for d, there in slots:
            remote(
                part.at[pl.ds(there * ch, ch)], rs.at[which, d],
                rs_send.at[which], rs_recv.at[which], (to_core, there, vec),
            ).start()

    def scatter_sent(which, first):
        count = (rows_n - first) * ch
        remote(
            part.at[pl.ds(0, count)], part.at[pl.ds(0, count)],
            rs_send.at[which], rs_recv.at[which], (other, row, vec),
        ).wait_send()

    def scatter_arrived(which, first):
        view = rs.at[which, pl.ds(first, rows_n - first)]
        remote(
            view, view, rs_send.at[which], rs_recv.at[which], (other, row, vec)
        ).wait_recv()

    def gather(which):
        mine = full.at[which, pl.ds(row * ch, ch)]

        for there in peers:
            remote(
                mine, mine, ag_send.at[which], ag_recv.at[which], (core, there, vec)
            ).start()
        view = full.at[which, pl.ds(0, (rows_n - 1) * ch)]
        done = remote(view, view, ag_send.at[which], ag_recv.at[which], (other, row, vec))
        done.wait_recv()
        done.wait_send()

    def sum_rows(which, between=lambda n: None):
        scatter(which, core, 1)
        scatter_arrived(which, 1)
        between(2)
        total = part[pl.ds(row * ch, ch), :]
        for d in range(1, rows_n):
            total = total + rs[which, d]
        full[which, pl.ds(row * ch, ch), :] = total
        scatter_sent(which, 1)
        gather(which)
        between(3)

    def by_mode(with_transposes):
        for i in range(modes):
            x = jnp.concatenate(
                [stage[h, pl.ds(i, rank, stride=modes), :] for h in range(rank // 128)], axis=1
            )
            at = slice(i * rank, (i + 1) * rank)
            ghi[at, :], glo[at, :] = split(x)
            if with_transposes:
                gthi[at, :], gtlo[at, :] = split(x.T)
            elif i % mh >= sent:
                to = (i % mh - sent) * rank
                gring[i // mh, 0, to : to + rank, :] = x

    def left_gram(z):
        zhi, zlo = split(z)
        zboth = jnp.concatenate([zhi, zlo], axis=1)
        total = None
        for i in range(modes // GROUP):
            at = slice(i * GROUP * rank, (i + 1) * GROUP * rank)
            r = dot(ghi[at, :], zboth)
            x = r[:, :kept] + r[:, kept:] + dot(glo[at, :], zhi)
            hi, lo = split(x)
            both = jnp.concatenate([hi, lo], axis=1)
            xcat[at, :] = both
            swapped = jnp.concatenate([lo, hi], axis=1)
            wide = beside(both, GROUP)
            term = dot_nt(wide, wide) + dot_nt(wide, beside(swapped, GROUP))
            total = term if total is None else total + term
        part[...] = total

    def whiten(yt):
        xs[...] = fdot_nt(yt, yt)
        eliminate(xs, kept, PANEL)
        return factors(xs, kept)[0]

    scale = math.sqrt(kept * modes * rows_n)

    def shape_cores(ft, side, first, end):
        fhi, flo = split(ft)
        for m in range(first, end):
            i = side * mh + m
            both = xcat[i * rank : (i + 1) * rank, :]
            r = dot(fhi, both)
            n = r[:, :kept] + r[:, kept:] + dot(flo, both[:, :kept])
            ring[side, 0, (m + 2) * kept : (m + 3) * kept, :] = n.T
            rounded_buf[pl.ds(i, kept, stride=modes), :] = n * scale
            hi, lo = split(n)
            line = jnp.concatenate([hi, lo], axis=1)
            at = i * 2 * kept
            nw[at : at + kept, :] = line
            nw[at + kept : at + 2 * kept, :] = line

    def ring_copies(side, k, pieces):
        to = lax.rem(vec + (1 if side == 0 else vecs - 1), vecs)
        return [
            remote(
                ring.at[side, k, pl.ds(at * kept, count * kept)],
                ring.at[side, k + 1, pl.ds(at * kept, count * kept)],
                ring_send.at[side, k, n], ring_recv.at[side, k, n], (core, row, to),
            )
            for n, (at, count) in enumerate(pieces)
        ]

    def ring_step(k, pieces):
        for n in range(len(pieces)):
            for side in (0, 1):
                ring_copies(side, k - 1, pieces)[n].wait_recv()
                if k < half:
                    ring_copies(side, k, pieces)[n].start()

    def ring_sent(pieces):
        for k in range(half):
            for side in (0, 1):
                for copy in ring_copies(side, k, pieces):
                    copy.wait_send()

    def gring_copy(side, k):
        to = lax.rem(vec + (1 if side == 0 else vecs - 1), vecs)
        return remote(
            gring.at[side, k], gring.at[side, k + 1],
            gring_send.at[side, k], gring_recv.at[side, k], (core, row, to),
        )

    def gring_step(k):
        for side in (0, 1):
            if k > 0:
                gring_copy(side, k - 1).wait_recv()
            if k < half:
                gring_copy(side, k).start()

    def z_copy(side, k):
        to = lax.rem(vec + (1 if side == 0 else vecs - 1), vecs)
        return remote(
            zt_ref if k == 0 else zall.at[side, k], zall.at[side, k + 1],
            z_send.at[side, k], z_recv.at[side, k], (core, row, to),
        )

    def z_sides(k):
        return (0,) if k == half - 1 else (0, 1)

    def z_step(k):
        for side in (0, 1):
            if k > 0 and side in z_sides(k - 1):
                z_copy(side, k - 1).wait_recv()
            if k < half and side in z_sides(k):
                z_copy(side, k).start()

    def early_maps(k):
        for side in (0, 1):
            zhi, zlo = split(zall[0 if k == half else side, k])
            for e in range(early):
                hi, lo = split(gring[side, k, e * rank : (e + 1) * rank, :])
                m = dot_nt(zhi, hi) + dot_nt(zhi, lo) + dot_nt(zlo, hi)
                at = slice(e * kept, (e + 1) * kept)
                mthi[side, at, :], mtlo[side, at, :] = split(m)

    def early_cores(k):
        for side in (0, 1):
            u = jnp.concatenate([ring[side, k, :kept, :], ring[side, k, kept : 2 * kept, :]], 1)
            uhi, ulo = split(u)
            m = mthi[side]
            ring[side, k, (2 + sent) * kept :, :] = (
                dot_nt(m, uhi) + dot_nt(m, ulo) + dot_nt(mtlo[side], uhi)
            )

    def carry_modes(side, k, et):
        hi, lo = split(et)
        line = jnp.concatenate([hi, lo], axis=1)
        weights = jnp.concatenate([line, line], axis=0)
        hi, lo = split(ring[side, k, 2 * kept :, :])
        r = dot(jnp.concatenate([hi, lo], axis=1), weights)
        hi, lo = split(r[:, :kept] + r[:, kept:])
        wide = beside(jnp.concatenate([hi, lo], axis=1), mh)
        at = side * mh * 2 * kept
        acc = dot(wide, nw[pl.ds(at, mh * 2 * kept), :])
        return acc[:, :kept] + acc[:, kept:]

    def up_at(k):
        return vecs - 1 if k == half else k

    def down_at(k):
        return 0 if k == 0 else vecs - 1 if k == half else half - 1 + k

    def swap_copy(k, side):
        to = lax.rem(vec + (vecs - k if side == 0 else k), vecs)
        return remote(
            xsend.at[k - 1, side], xrecv.at[k - 1, side], x_send.at[k - 1], x_recv.at[k - 1],
            (core, row, to),
        )

    def margin_work(k, env):
        first = carry_modes(0, k, env(0, k))
        second = carry_modes(1, k, env(1, k))
        if k == 0 or k == half:
            epart[up_at(k)] = first + second
        else:
            epart[down_at(k)] = first
            epart[up_at(k)] = second
            xsend[k - 1, 0] = first.T
            xsend[k - 1, 1] = second.T
            for side in (0, 1):
                swap_copy(k, side).start()

    def swap_done():
        for k in range(1, half):
            view = xrecv.at[k - 1]
            done = remote(view, view, x_send.at[k - 1], x_recv.at[k - 1], (other, row, vec))
            done.wait_recv()
            done.wait_send()
            epart[up_at(k)] += xrecv[k - 1, 0]
            epart[down_at(k)] += xrecv[k - 1, 1]

    spans = ((0, vecs - 1), (vecs - 1, 1))

    def margin_scatter(g):
        first, count = spans[g]

        for d, there in enumerate(peers, 1):
            remote(
                epart.at[pl.ds(first, count), pl.ds(there * ech, ech), :],
                ers.at[d, pl.ds(first, count)],
                ers_send.at[g], ers_recv.at[g], (core, there, vec),
            ).start()

    def margin_gather(g):
        first, count = spans[g]
        view = ers.at[pl.ds(1, rows_n - 1), pl.ds(first, count)]
        done = remote(view, view, ers_send.at[g], ers_recv.at[g], (other, row, vec))
        done.wait_recv()
        mine = pl.ds(pl.multiple_of(row * ech, ech), ech)
        total = epart[pl.ds(first, count), mine, :]
        for d in range(1, rows_n):
            total = total + ers[d, pl.ds(first, count)]
        efull[pl.ds(first, count), mine, :] = total
        chunk = efull.at[pl.ds(first, count), mine, :]

        for there in peers:
            remote(
                chunk, chunk, eag_send.at[g], eag_recv.at[g], (core, there, vec)
            ).start()
        done.wait_send()

    def margin_gathered(g):
        first, count = spans[g]
        view = efull.at[pl.ds(first, count), pl.ds(0, (rows_n - 1) * ech), :]
        done = remote(view, view, eag_send.at[g], eag_recv.at[g], (other, row, vec))
        done.wait_recv()
        done.wait_send()

    def margin_pair(g):
        first, count = spans[g]
        span = pl.ds(first, count)
        return pair_copy(efull.at[span], ein.at[span], 3 + g)

    def margins_out(g):
        first, count = spans[g]
        for at in range(first, first + count):
            away = at if at < half else at - half + 1
            shift = half if at == vecs - 1 else at if at < half else vecs - away
            q = lax.rem(vec + shift, vecs)
            lanes = pl.ds(pl.multiple_of(q * kept, kept), kept)
            margins_buf[:, lanes] = efull[at].T

    out_copies = [
        pltpu.make_async_copy(rounded_buf, rounded_ref, out_sem.at[0]),
        pltpu.make_async_copy(bases_buf, bases_ref, out_sem.at[1]),
        pltpu.make_async_copy(margins_buf, margins_ref, out_sem.at[2]),
    ]

    bases_scale = math.sqrt(rank)

    @pl.when(core == 0)
    def front():
        part[...] = jnp.zeros_like(part)
        full[0] = jnp.zeros_like(part)
        for t in range(pieces):
            for h in range(rank // 128):
                loads[t * (rank // 128) + h].wait()
            hi, lo = split(
                jnp.concatenate(
                    [stage[h, pl.ds(t * prow, prow), :] for h in range(rank // 128)], axis=1
                )
            )
            part[...] += dot_tn(hi, hi)
            full[2] = dot_tn(hi, lo) if t == 0 else full[2] + dot_tn(hi, lo)
        cross = full[2]
        part[...] += cross + cross.T
        meet()
        scatter(0, other, 0)
        by_mode(False)
        gring_step(0)
        wt = w_ref[...].T
        scatter_sent(0, 0)

        pair_copy(full.at[0], full.at[0], 0).wait_recv()
        gring_step(1)
        xs[...] = full[0, :kept, :kept]
        eliminate(xs, kept, PANEL, unrolled=False)
        kinv, kt = factors(xs, kept)
        if half > 2:
            gring_step(2)
        lower_ref[:kept, :kept] = kt.T
        lower_ref[:kept, kept:] = jnp.zeros((kept, rank - kept), F32)
        left = fdot_nt(full[0, kept:, :kept], kinv)
        lower_ref[kept:, :kept] = left
        xs[...] = full[0, kept:, kept:] - fdot_nt(left, left)
        eliminate(xs, kept, PANEL, unrolled=False)
        kinv, kt = factors(xs, kept)
        lower_ref[kept:, kept:] = kt.T
        to_pair = pair_copy(lower_ref, lower_ref, 1)
        to_pair.start()

        for k in range(3, half):
            gring_step(k)
        pair_copy(zt_ref, zt_ref, 2).wait_recv()
        z_step(0)
        left_gram(zt_ref[...].T)
        z_step(1)
        sum_rows(1, lambda n: z_step(n) if 1 < n < half else None)
        gram = full[1]
        yt = fdot(fdot(wt, gram), gram)
        ut = fdot(whiten(yt), yt)
        bases_buf[...] = ut.T * bases_scale
        out_copies[1].start()
        cuts = [(0, 2), (2, sent)]
        for side in (0, 1):
            ring[side, 0, :kept, :] = ut[:, :kept]
            ring[side, 0, kept : 2 * kept, :] = ut[:, kept:]
            ring_copies(side, 0, cuts)[0].start()
        for side in (0, 1):
            shape_cores(ut, side, 0, sent)
            ring_copies(side, 0, cuts)[1].start()
        for side in (0, 1):
            shape_cores(ut, side, sent, mh)
        out_copies[0].start()
        gring_step(half)
        z_step(half)

        def env(side, k):
            a = ring[side, k, :kept, :]
            b = ring[side, k, kept : 2 * kept, :]
            c = ring[0, 0, :kept, :]
            d = ring[0, 0, kept : 2 * kept, :]
            return fdot_nt(a, c) + fdot_nt(b, d)

        margin_work(0, env)
        for k in range(1, half):
            early_maps(k)
            ring_step(k, cuts)
            early_cores(k)
            margin_work(k, env)
        early_maps(half)
        swap_done()
        margin_scatter(0)
        margin_gather(0)
        ring_step(half, cuts)
        early_cores(half)
        margin_work(half, env)
        margin_scatter(1)
        margin_gathered(0)
        margin_pair(0).start()
        margin_gather(1)
        margins_out(0)
        margin_gathered(1)
        margin_pair(1).start()
        margins_out(1)
        out_copies[2].start()
        ring_sent(cuts)
        for k in range(half):
            for side in z_sides(k):
                z_copy(side, k).wait_send()
            for side in (0, 1):
                gring_copy(side, k).wait_send()
        to_pair.wait_send()
        margin_pair(0).wait_send()
        margin_pair(1).wait_send()
        for copy in out_copies:
            copy.wait()

    @pl.when(core == 1)
    def back():
        for load in loads:
            load.wait()
        by_mode(True)
        wt = w_ref[...].T
        xwt = xw_ref[...].T
        meet()
        scatter_arrived(0, 0)
        total = rs[0, 0]
        for d in range(1, rows_n):
            total = total + rs[0, d]
        full[0, pl.ds(row * ch, ch), :] = total
        gather(0)
        to_pair = pair_copy(full.at[0], full.at[0], 0)
        to_pair.start()

        chi, clo = split(full[0])
        cboth = jnp.concatenate([chi, clo], axis=1)
        total = None
        for i in range(modes // GROUP):
            at = slice(i * GROUP * rank, (i + 1) * GROUP * rank)
            r = dot(gthi[at, :], cboth)
            h = r[:, :rank] + r[:, rank:] + dot(gtlo[at, :], chi)
            hi, lo = split(h)
            hi = beside(hi, GROUP)
            g = ghi[at, :]
            term = dot(hi, g) + dot(hi, glo[at, :]) + dot(beside(lo, GROUP), g)
            total = term if total is None else total + term
        part[...] = total
        sum_rows(1)
        gram = full[1]
        yt = fdot(fdot(xwt, gram), gram)
        ut = fdot(whiten(yt), yt)
        left_gram(ut.T)
        sum_rows(2)

        pair_copy(lower_ref, lower_ref, 1).wait_recv()
        low = lower_ref[...]
        vt = fdot_nt(wt, low)
        pt = fdot(fdot(fdot(vt, full[2]), full[0]), full[2])
        yt = fdot(pt, low)
        kinv = whiten(yt)
        zt_ref[...] = fdot(kinv, pt)
        z_pair = pair_copy(zt_ref, zt_ref, 2)
        z_pair.start()
        ut = fdot(kinv, yt)
        bases_buf[...] = ut.T * bases_scale
        out_copies[1].start()
        ft = fdot_nt(ut, low)
        cuts = [(2, sent), (2 + sent, early)]
        for side in (0, 1):
            shape_cores(ft, side, 0, mh)
            for copy in ring_copies(side, 0, cuts):
                copy.start()
        out_copies[0].start()
        for k in range(1, half + 1):
            ring_step(k, cuts)

        def env(side, k):
            return ein[down_at(k) if side == 0 else up_at(k)]

        margin_pair(0).wait_recv()
        for k in range(half - 1, -1, -1):
            margin_work(k, env)
        swap_done()
        margin_scatter(0)
        margin_pair(1).wait_recv()
        margin_work(half, env)
        margin_scatter(1)
        margin_gather(0)
        margin_gather(1)
        margin_gathered(0)
        margins_out(0)
        margin_gathered(1)
        margins_out(1)
        out_copies[2].start()
        ring_sent(cuts)
        to_pair.wait_send()
        z_pair.wait_send()
        for copy in out_copies:
            copy.wait()


def deliver(*refs):
    sources, targets, buffers = refs[:3], refs[3:6], refs[6:9]
    into, out = refs[9:]
    spans = [
        (n, pl.ds(t * (src.shape[0] // count), src.shape[0] // count))
        for n, (src, count) in enumerate(zip(sources, (4, 1, 2)))
        for t in range(count)
    ]
    loads = [
        pltpu.make_async_copy(sources[n].at[span], buffers[n].at[span], into.at[t])
        for t, (n, span) in enumerate(spans)
    ]
    stores = [
        pltpu.make_async_copy(buffers[n].at[span], targets[n].at[span], out.at[t])
        for t, (n, span) in enumerate(spans)
    ]
    for copy in loads:
        copy.start()
    for load, store in zip(loads, stores):
        load.wait()
        store.start()
    for store in stores:
        store.wait()


def build(mesh):
    rows_n = mesh.shape["row"]
    vecs = mesh.shape["vec"]

    def local(train_cores, sketch, exit_sketch):
        _, rank, modes, _ = train_cores.shape
        kept = sketch.shape[1]
        half = vecs // 2
        mh = modes // 2
        early = EARLY if mh > EARLY else mh // 2
        ch = rank // rows_n
        ech = kept // rows_n
        dma = pltpu.SemaphoreType.DMA
        vmem = pl.BlockSpec(memory_space=pltpu.VMEM)
        shapes = (
            jax.ShapeDtypeStruct((kept * modes, kept), F32),
            jax.ShapeDtypeStruct((rank, kept), F32),
            jax.ShapeDtypeStruct((kept, vecs * kept), F32),
        )
        hbm = pl.BlockSpec(memory_space=pl.ANY)
        results = pl.pallas_call(
            functools.partial(kernel, (rank, kept, modes, rows_n, vecs)),
            out_shape=shapes,
            in_specs=[hbm, vmem, vmem],
            out_specs=(hbm, hbm, hbm),
            scratch_shapes=[
                pltpu.VMEM((rank // 128, rank * modes, 128), F32),
                pltpu.VMEM((modes * rank, rank), BF16),
                pltpu.VMEM((modes * rank, rank), BF16),
                pltpu.VMEM((modes * rank, rank), BF16),
                pltpu.VMEM((modes * rank, rank), BF16),
                pltpu.VMEM((rank, rank), F32),
                pltpu.VMEM((3, rows_n, ch, rank), F32),
                pltpu.VMEM((3, rank, rank), F32),
                pltpu.VMEM((rank, rank), F32),
                pltpu.VMEM((kept, rank), F32),
                pltpu.VMEM((kept, kept), F32),
                pltpu.VMEM((modes * rank, 2 * kept), BF16),
                pltpu.VMEM((modes * 2 * kept, 2 * kept), BF16),
                pltpu.VMEM((2, half + 1, (mh + 2) * kept, kept), F32),
                pltpu.VMEM((vecs, kept, kept), F32),
                pltpu.VMEM((rows_n, vecs, ech, kept), F32),
                pltpu.VMEM((half - 1, 2, kept, kept), F32),
                pltpu.VMEM((half - 1, 2, kept, kept), F32),
                pltpu.VMEM((vecs, kept, kept), F32),
                pltpu.VMEM((vecs, kept, kept), F32),
                pltpu.VMEM((kept * modes, kept), F32),
                pltpu.VMEM((rank, kept), F32),
                pltpu.VMEM((kept, vecs * kept), F32),
                dma((8, rank // 128)),
                dma((3,)), dma((3,)), dma((3,)), dma((3,)),
                dma((5,)), dma((5,)),
                dma((2, half, 2)), dma((2, half, 2)),
                dma((2,)), dma((2,)), dma((half - 1,)), dma((half - 1,)), dma((2,)), dma((2,)),
                dma((3,)),
                pltpu.VMEM((2, half + 1, early * rank, rank), F32),
                pltpu.VMEM((2, half + 1, kept, rank), F32),
                pltpu.VMEM((2, early * kept, rank), BF16),
                pltpu.VMEM((2, early * kept, rank), BF16),
                dma((2, half)), dma((2, half)), dma((2, half)), dma((2, half)),
            ],
            compiler_params=pltpu.CompilerParams(
                collective_id=0, has_side_effects=True, vmem_limit_bytes=58 * 1024 * 1024
            ),
        )(train_cores.reshape(rank * modes, rank), sketch, exit_sketch)
        rounded, bases, margins = pl.pallas_call(
            deliver,
            out_shape=shapes,
            in_specs=[hbm] * 3,
            out_specs=(hbm, hbm, hbm),
            scratch_shapes=[pltpu.VMEM(x.shape, F32) for x in shapes] + [dma((7,)), dma((7,))],
        )(*results)
        return (
            rounded.reshape(1, kept, modes, kept),
            bases[None],
            margins[None],
        )

    return local


def solution(mesh):
    return jax.shard_map(
        build(mesh),
        mesh=mesh,
        in_specs=(P("vec", "cores", "row", None), P("cores", None), P()),
        out_specs=(
            P("vec", "cores", "row", None),
            P("vec", "cores", None),
            P("vec", "cores", None),
        ),
        check_vma=False,
    )
```

```python
import functools
import math

import jax
import jax.numpy as jnp
from jax import lax
from jax.experimental import pallas as pl
from jax.experimental.pallas import tpu as pltpu
from jax.sharding import PartitionSpec as P

MESH = pl.DeviceIdType.MESH
F32 = jnp.float32
BF16 = jnp.bfloat16
HIGHEST = lax.Precision.HIGHEST
PANEL = 16
GROUP = 2
EARLY = 3


def dot(a, b):
    return jnp.dot(a, b, preferred_element_type=F32)


def dot_nt(a, b):
    return lax.dot_general(a, b, (((1,), (1,)), ((), ())), preferred_element_type=F32)


def dot_tn(a, b):
    return lax.dot_general(a, b, (((0,), (0,)), ((), ())), preferred_element_type=F32)


def fdot(a, b):
    return jnp.dot(a, b, precision=HIGHEST, preferred_element_type=F32)


def fdot_nt(a, b):
    return lax.dot_general(
        a, b, (((1,), (1,)), ((), ())), precision=HIGHEST, preferred_element_type=F32
    )


def fdot_tn(a, b):
    return lax.dot_general(
        a, b, (((0,), (0,)), ((), ())), precision=HIGHEST, preferred_element_type=F32
    )


def split(x):
    hi = x.astype(BF16)
    lo = (x - hi.astype(F32)).astype(BF16)
    return hi, lo


def beside(x, count):
    n = x.shape[0] // count
    return jnp.concatenate([x[m * n : (m + 1) * n] for m in range(count)], axis=1)


def three(x):
    a = x.astype(BF16)
    rest = x - a.astype(F32)
    b = rest.astype(BF16)
    return a, b, (rest - b.astype(F32)).astype(BF16)


def eliminate(xs, n, nb, unrolled=True):
    lane = lax.broadcasted_iota(jnp.int32, (nb, n), 1)
    sub = lax.broadcasted_iota(jnp.int32, (nb, n), 0)

    def panel(t, carry):
        if unrolled:
            j0 = t * nb
            v = xs[j0 : j0 + nb, :]
            square = v[:, j0 : j0 + nb]
        else:
            j0 = pl.multiple_of(t * nb, nb)
            v = xs[pl.ds(j0, nb), :]
            square = pltpu.roll(v, lax.rem(n - j0, n), 1)[:, :nb]
        cols = jnp.stack([jnp.broadcast_to(square[:, k : k + 1], (nb, n)) for k in range(nb)])
        inv = jnp.zeros((nb, n), F32)
        for k in range(nb):
            rp = jnp.broadcast_to(1.0 / cols[0, k : k + 1, :], (nb, n))
            inv = jnp.where(sub == k, rp, inv)
            f = jnp.where(sub > k, cols[0] * rp, 0.0)
            if k + 1 < nb:
                cols = cols[1:]
                cols = cols - f[None] * cols[:, k : k + 1, :]
            pivot_row = v[k : k + 1, :]
            pivot_row = jnp.where(lane[:1] == j0 + k, 2.0 * pivot_row, pivot_row)
            v = v - f * pivot_row
        below = jnp.where(lane >= j0 + nb, v, 0.0)
        scaled = jnp.where(lane == j0 + sub, 2.0 * v, v) * inv
        a, b, c = three(below)
        d, e, g = three(scaled)
        update = dot_tn(
            jnp.concatenate([a, a, b, a, b, c], axis=0), jnp.concatenate([d, e, d, g, e, d], axis=0)
        )
        xs[...] = xs[...] - update
        xs[pl.ds(j0, nb), :] = v
        return carry

    if unrolled:
        for t in range(n // nb):
            panel(t, 0)
    else:
        lax.fori_loop(0, n // nb, panel, 0)


def factors(xs, n):
    x = xs[...]
    rows = lax.broadcasted_iota(jnp.int32, (n, n), 0)
    lanes = lax.broadcasted_iota(jnp.int32, (n, n), 1)
    diag = jnp.where(rows == lanes, x, 0.0)
    by_row = 1.0 / jnp.sqrt(jnp.sum(diag, axis=1, keepdims=True))
    by_lane = 1.0 / jnp.sum(diag, axis=0, keepdims=True)
    lower = jnp.where(rows > lanes, x * by_lane, jnp.where(rows == lanes, 1.0, 0.0))
    upper = jnp.where(rows <= lanes, x, 0.0)
    return lower * by_row, upper * by_row


def kernel(
    sizes,
    g_hbm, w_ref, xw_ref,
    rounded_ref, bases_ref, margins_ref,
    stage, ghi, glo, gthi, gtlo, part, rs, full, lower_ref, zt_ref, xs, xcat, nw,
    ring, epart, ers, xsend, xrecv, efull, ein, rounded_buf, bases_buf, margins_buf,
    load_sem, rs_send, rs_recv, ag_send, ag_recv, pair_send, pair_recv,
    ring_send, ring_recv, ers_send, ers_recv, x_send, x_recv, eag_send, eag_recv, out_sem,
    gring, zall, mthi, mtlo, gring_send, gring_recv, z_send, z_recv, turn,
):
    rank, kept, modes, rows_n, vecs = sizes
    half = vecs // 2
    mh = modes // 2
    ch = rank // rows_n
    ech = kept // rows_n
    early = EARLY if mh > EARLY else mh // 2
    sent = mh - early
    core = lax.axis_index("cores")
    row = lax.axis_index("row")
    vec = lax.axis_index("vec")
    other = 1 - core

    side_n = math.isqrt(rows_n)
    if side_n * side_n == rows_n and side_n > 2:
        offsets = [(a, b) for a in range(side_n) for b in range(side_n) if a or b]
        offsets.sort(key=lambda o: -sum(min(v, side_n - v) for v in o))
        peers = [
            lax.rem(row // side_n + a, side_n) * side_n + lax.rem(row % side_n + b, side_n)
            for a, b in offsets
        ]
    else:
        peers = [lax.rem(row + d, rows_n) for d in range(1, rows_n)]

    pieces = load_sem.shape[0]
    prow = rank * modes // pieces
    loads = [
        pltpu.make_async_copy(
            g_hbm.at[pl.ds(t * prow, prow), pl.ds(h * 128, 128)],
            stage.at[h, pl.ds(t * prow, prow)],
            load_sem.at[t, h],
        )
        for t in range(pieces)
        for h in range(rank // 128)
    ]
    for load in loads:
        load.start()

    barrier = pltpu.get_barrier_semaphore()

    def greet(d, carry):
        there = lax.rem(row + d, rows_n)
        pl.semaphore_signal(barrier, inc=1, device_id=(core, there, vec), device_id_type=MESH)
        pl.semaphore_signal(barrier, inc=1, device_id=(other, there, vec), device_id_type=MESH)
        return carry

    lax.fori_loop(1, rows_n, greet, 0)
    pl.semaphore_signal(barrier, inc=1, device_id=(other, row, vec), device_id_type=MESH)
    for d in range(1, vecs):
        pl.semaphore_signal(
            barrier, inc=1, device_id=(core, row, lax.rem(vec + d, vecs)), device_id_type=MESH
        )

    def meet():
        pl.semaphore_wait(barrier, 2 * (rows_n - 1) + 1 + vecs - 1)

    def remote(src, dst, send, recv, to):
        return pltpu.make_async_remote_copy(
            src_ref=src, dst_ref=dst, send_sem=send, recv_sem=recv,
            device_id=to, device_id_type=MESH,
        )

    def pair_copy(src, dst, which):
        return remote(src, dst, pair_send.at[which], pair_recv.at[which], (other, row, vec))

    def scatter(which, to_core, first):
        slots = [(d + 1, there) for d, there in enumerate(peers)]
        if first == 0:
            slots.append((0, row))
        for d, there in slots:
            remote(
                part.at[pl.ds(there * ch, ch)], rs.at[which, d],
                rs_send.at[which], rs_recv.at[which], (to_core, there, vec),
            ).start()

    def scatter_sent(which, first):
        count = (rows_n - first) * ch
        remote(
            part.at[pl.ds(0, count)], part.at[pl.ds(0, count)],
            rs_send.at[which], rs_recv.at[which], (other, row, vec),
        ).wait_send()

    def scatter_arrived(which, first):
        view = rs.at[which, pl.ds(first, rows_n - first)]
        remote(
            view, view, rs_send.at[which], rs_recv.at[which], (other, row, vec)
        ).wait_recv()

    def gather(which):
        mine = full.at[which, pl.ds(row * ch, ch)]

        for there in peers:
            remote(
                mine, mine, ag_send.at[which], ag_recv.at[which], (core, there, vec)
            ).start()
        view = full.at[which, pl.ds(0, (rows_n - 1) * ch)]
        done = remote(view, view, ag_send.at[which], ag_recv.at[which], (other, row, vec))
        done.wait_recv()
        done.wait_send()

    def sum_rows(which, between=lambda n: None):
        scatter(which, core, 1)
        scatter_arrived(which, 1)
        between(2)
        total = part[pl.ds(row * ch, ch), :]
        for d in range(1, rows_n):
            total = total + rs[which, d]
        full[which, pl.ds(row * ch, ch), :] = total
        scatter_sent(which, 1)
        gather(which)
        between(3)

    def by_mode(with_transposes):
        for i in range(modes):
            x = jnp.concatenate(
                [stage[h, pl.ds(i, rank, stride=modes), :] for h in range(rank // 128)], axis=1
            )
            at = slice(i * rank, (i + 1) * rank)
            ghi[at, :], glo[at, :] = split(x)
            if with_transposes:
                gthi[at, :], gtlo[at, :] = split(x.T)
            elif i % mh >= sent:
                to = (i % mh - sent) * rank
                gring[i // mh, 0, to : to + rank, :] = x

    def left_gram(z):
        zhi, zlo = split(z)
        zboth = jnp.concatenate([zhi, zlo], axis=1)
        total = None
        for i in range(modes // GROUP):
            at = slice(i * GROUP * rank, (i + 1) * GROUP * rank)
            r = dot(ghi[at, :], zboth)
            x = r[:, :kept] + r[:, kept:] + dot(glo[at, :], zhi)
            hi, lo = split(x)
            both = jnp.concatenate([hi, lo], axis=1)
            xcat[at, :] = both
            swapped = jnp.concatenate([lo, hi], axis=1)
            wide = beside(both, GROUP)
            term = dot_nt(wide, wide) + dot_nt(wide, beside(swapped, GROUP))
            total = term if total is None else total + term
        part[...] = total

    def whiten(yt):
        xs[...] = fdot_nt(yt, yt)
        eliminate(xs, kept, PANEL)
        return factors(xs, kept)[0]

    scale = math.sqrt(kept * modes * rows_n)

    def shape_cores(ft, side, first, end):
        fhi, flo = split(ft)
        for m in range(first, end):
            i = side * mh + m
            both = xcat[i * rank : (i + 1) * rank, :]
            r = dot(fhi, both)
            n = r[:, :kept] + r[:, kept:] + dot(flo, both[:, :kept])
            ring[side, 0, (m + 2) * kept : (m + 3) * kept, :] = n.T
            rounded_buf[pl.ds(i, kept, stride=modes), :] = n * scale
            hi, lo = split(n)
            line = jnp.concatenate([hi, lo], axis=1)
            at = i * 2 * kept
            nw[at : at + kept, :] = line
            nw[at + kept : at + 2 * kept, :] = line

    def ring_copies(side, k, pieces):
        to = lax.rem(vec + (1 if side == 0 else vecs - 1), vecs)
        return [
            remote(
                ring.at[side, k, pl.ds(at * kept, count * kept)],
                ring.at[side, k + 1, pl.ds(at * kept, count * kept)],
                ring_send.at[side, k, n], ring_recv.at[side, k, n], (core, row, to),
            )
            for n, (at, count) in enumerate(pieces)
        ]

    def ring_step(k, pieces):
        for n in range(len(pieces)):
            for side in (0, 1):
                ring_copies(side, k - 1, pieces)[n].wait_recv()
                if k < half:
                    ring_copies(side, k, pieces)[n].start()

    def ring_sent(pieces):
        for k in range(half):
            for side in (0, 1):
                for copy in ring_copies(side, k, pieces):
                    copy.wait_send()

    def gring_copy(side, k):
        to = lax.rem(vec + (1 if side == 0 else vecs - 1), vecs)
        return remote(
            gring.at[side, k], gring.at[side, k + 1],
            gring_send.at[side, k], gring_recv.at[side, k], (core, row, to),
        )

    def gring_step(k):
        for side in (0, 1):
            if k > 0:
                gring_copy(side, k - 1).wait_recv()
            if k < half:
                gring_copy(side, k).start()

    def z_copy(side, k):
        to = lax.rem(vec + (1 if side == 0 else vecs - 1), vecs)
        return remote(
            zt_ref if k == 0 else zall.at[side, k], zall.at[side, k + 1],
            z_send.at[side, k], z_recv.at[side, k], (core, row, to),
        )

    def z_sides(k):
        return (0,) if k == half - 1 else (0, 1)

    def z_step(k):
        for side in (0, 1):
            if k > 0 and side in z_sides(k - 1):
                z_copy(side, k - 1).wait_recv()
            if k < half and side in z_sides(k):
                z_copy(side, k).start()

    def early_maps(k):
        for side in (0, 1):
            zhi, zlo = split(zall[0 if k == half else side, k])
            for e in range(early):
                hi, lo = split(gring[side, k, e * rank : (e + 1) * rank, :])
                m = dot_nt(zhi, hi) + dot_nt(zhi, lo) + dot_nt(zlo, hi)
                at = slice(e * kept, (e + 1) * kept)
                mthi[side, at, :], mtlo[side, at, :] = split(m)

    def early_cores(k):
        for side in (0, 1):
            u = jnp.concatenate([ring[side, k, :kept, :], ring[side, k, kept : 2 * kept, :]], 1)
            uhi, ulo = split(u)
            m = mthi[side]
            ring[side, k, (2 + sent) * kept :, :] = (
                dot_nt(m, uhi) + dot_nt(m, ulo) + dot_nt(mtlo[side], uhi)
            )

    def carry_modes(side, k, et):
        hi, lo = split(et)
        line = jnp.concatenate([hi, lo], axis=1)
        weights = jnp.concatenate([line, line], axis=0)
        hi, lo = split(ring[side, k, 2 * kept :, :])
        r = dot(jnp.concatenate([hi, lo], axis=1), weights)
        hi, lo = split(r[:, :kept] + r[:, kept:])
        wide = beside(jnp.concatenate([hi, lo], axis=1), mh)
        at = side * mh * 2 * kept
        acc = dot(wide, nw[pl.ds(at, mh * 2 * kept), :])
        return acc[:, :kept] + acc[:, kept:]

    def up_at(k):
        return vecs - 1 if k == half else k

    def down_at(k):
        return 0 if k == 0 else vecs - 1 if k == half else half - 1 + k

    def swap_copy(k, side):
        to = lax.rem(vec + (vecs - k if side == 0 else k), vecs)
        return remote(
            xsend.at[k - 1, side], xrecv.at[k - 1, side], x_send.at[k - 1], x_recv.at[k - 1],
            (core, row, to),
        )

    def margin_work(k, env):
        first = carry_modes(0, k, env(0, k))
        second = carry_modes(1, k, env(1, k))
        if k == 0 or k == half:
            epart[up_at(k)] = first + second
        else:
            epart[down_at(k)] = first
            epart[up_at(k)] = second
            xsend[k - 1, 0] = first.T
            xsend[k - 1, 1] = second.T
            for side in (0, 1):
                swap_copy(k, side).start()

    def swap_done():
        for k in range(1, half):
            view = xrecv.at[k - 1]
            done = remote(view, view, x_send.at[k - 1], x_recv.at[k - 1], (other, row, vec))
            done.wait_recv()
            done.wait_send()
            epart[up_at(k)] += xrecv[k - 1, 0]
            epart[down_at(k)] += xrecv[k - 1, 1]

    spans = ((0, vecs - 1), (vecs - 1, 1))

    def margin_scatter(g):
        first, count = spans[g]

        for d, there in enumerate(peers, 1):
            remote(
                epart.at[pl.ds(first, count), pl.ds(there * ech, ech), :],
                ers.at[d, pl.ds(first, count)],
                ers_send.at[g], ers_recv.at[g], (core, there, vec),
            ).start()

    def margin_gather(g):
        first, count = spans[g]
        view = ers.at[pl.ds(1, rows_n - 1), pl.ds(first, count)]
        done = remote(view, view, ers_send.at[g], ers_recv.at[g], (other, row, vec))
        done.wait_recv()
        mine = pl.ds(pl.multiple_of(row * ech, ech), ech)
        total = epart[pl.ds(first, count), mine, :]
        for d in range(1, rows_n):
            total = total + ers[d, pl.ds(first, count)]
        efull[pl.ds(first, count), mine, :] = total
        chunk = efull.at[pl.ds(first, count), mine, :]

        for there in peers:
            remote(
                chunk, chunk, eag_send.at[g], eag_recv.at[g], (core, there, vec)
            ).start()
        done.wait_send()

    def margin_gathered(g):
        first, count = spans[g]
        view = efull.at[pl.ds(first, count), pl.ds(0, (rows_n - 1) * ech), :]
        done = remote(view, view, eag_send.at[g], eag_recv.at[g], (other, row, vec))
        done.wait_recv()
        done.wait_send()

    def margin_pair(g):
        first, count = spans[g]
        span = pl.ds(first, count)
        return pair_copy(efull.at[span], ein.at[span], 3 + g)

    def margins_out(g):
        first, count = spans[g]
        for at in range(first, first + count):
            away = at if at < half else at - half + 1
            shift = half if at == vecs - 1 else at if at < half else vecs - away
            q = lax.rem(vec + shift, vecs)
            lanes = pl.ds(pl.multiple_of(q * kept, kept), kept)
            margins_buf[:, lanes] = efull[at].T

    out_copies = [
        pltpu.make_async_copy(rounded_buf, rounded_ref, out_sem.at[0]),
        pltpu.make_async_copy(bases_buf, bases_ref, out_sem.at[1]),
        pltpu.make_async_copy(margins_buf, margins_ref, out_sem.at[2]),
    ]

    bases_scale = math.sqrt(rank)

    @pl.when(core == 0)
    def front():
        part[...] = jnp.zeros_like(part)
        full[0] = jnp.zeros_like(part)
        for t in range(pieces):
            for h in range(rank // 128):
                loads[t * (rank // 128) + h].wait()
            hi, lo = split(
                jnp.concatenate(
                    [stage[h, pl.ds(t * prow, prow), :] for h in range(rank // 128)], axis=1
                )
            )
            part[...] += dot_tn(hi, hi)
            full[2] = dot_tn(hi, lo) if t == 0 else full[2] + dot_tn(hi, lo)
        cross = full[2]
        part[...] += cross + cross.T
        meet()
        scatter(0, other, 0)
        by_mode(False)
        gring_step(0)
        wt = w_ref[...].T
        scatter_sent(0, 0)

        pair_copy(full.at[0], full.at[0], 0).wait_recv()
        gring_step(1)
        xs[...] = full[0, :kept, :kept]
        eliminate(xs, kept, PANEL, unrolled=False)
        kinv, kt = factors(xs, kept)
        if half > 2:
            gring_step(2)
        lower_ref[:kept, :kept] = kt.T
        lower_ref[:kept, kept:] = jnp.zeros((kept, rank - kept), F32)
        left = fdot_nt(full[0, kept:, :kept], kinv)
        lower_ref[kept:, :kept] = left
        xs[...] = full[0, kept:, kept:] - fdot_nt(left, left)
        eliminate(xs, kept, PANEL, unrolled=False)
        kinv, kt = factors(xs, kept)
        lower_ref[kept:, kept:] = kt.T
        to_pair = pair_copy(lower_ref, lower_ref, 1)
        to_pair.start()

        for k in range(3, half):
            gring_step(k)
        pair_copy(zt_ref, zt_ref, 2).wait_recv()
        z_step(0)
        left_gram(zt_ref[...].T)
        z_step(1)
        sum_rows(1, lambda n: z_step(n) if 1 < n < half else None)
        gram = full[1]
        yt = fdot(fdot(wt, gram), gram)
        ut = fdot(whiten(yt), yt)
        bases_buf[...] = ut.T * bases_scale
        out_copies[1].start()
        cuts = [(0, 2), (2, sent)]
        for side in (0, 1):
            ring[side, 0, :kept, :] = ut[:, :kept]
            ring[side, 0, kept : 2 * kept, :] = ut[:, kept:]
            ring_copies(side, 0, cuts)[0].start()
        for side in (0, 1):
            shape_cores(ut, side, 0, sent)
            ring_copies(side, 0, cuts)[1].start()
        for side in (0, 1):
            shape_cores(ut, side, sent, mh)
        out_copies[0].start()
        gring_step(half)
        z_step(half)

        def env(side, k):
            a = ring[side, k, :kept, :]
            b = ring[side, k, kept : 2 * kept, :]
            c = ring[0, 0, :kept, :]
            d = ring[0, 0, kept : 2 * kept, :]
            return fdot_nt(a, c) + fdot_nt(b, d)

        margin_work(0, env)
        for k in range(1, half):
            early_maps(k)
            ring_step(k, cuts)
            early_cores(k)
            margin_work(k, env)
        early_maps(half)
        swap_done()
        margin_scatter(0)
        margin_gather(0)
        ring_step(half, cuts)
        pl.semaphore_signal(turn, inc=1, device_id=(other, row, vec), device_id_type=MESH)
        early_cores(half)
        margin_work(half, env)
        margin_scatter(1)
        margin_gathered(0)
        margin_pair(0).start()
        margin_gather(1)
        margins_out(0)
        margin_gathered(1)
        margin_pair(1).start()
        margins_out(1)
        out_copies[2].start()
        ring_sent(cuts)
        for k in range(half):
            for side in z_sides(k):
                z_copy(side, k).wait_send()
            for side in (0, 1):
                gring_copy(side, k).wait_send()
        to_pair.wait_send()
        margin_pair(0).wait_send()
        margin_pair(1).wait_send()
        for copy in out_copies:
            copy.wait()

    @pl.when(core == 1)
    def back():
        for load in loads:
            load.wait()
        by_mode(True)
        wt = w_ref[...].T
        xwt = xw_ref[...].T
        meet()
        scatter_arrived(0, 0)
        total = rs[0, 0]
        for d in range(1, rows_n):
            total = total + rs[0, d]
        full[0, pl.ds(row * ch, ch), :] = total
        gather(0)
        to_pair = pair_copy(full.at[0], full.at[0], 0)
        to_pair.start()

        chi, clo = split(full[0])
        cboth = jnp.concatenate([chi, clo], axis=1)
        total = None
        for i in range(modes // GROUP):
            at = slice(i * GROUP * rank, (i + 1) * GROUP * rank)
            r = dot(gthi[at, :], cboth)
            h = r[:, :rank] + r[:, rank:] + dot(gtlo[at, :], chi)
            hi, lo = split(h)
            hi = beside(hi, GROUP)
            g = ghi[at, :]
            term = dot(hi, g) + dot(hi, glo[at, :]) + dot(beside(lo, GROUP), g)
            total = term if total is None else total + term
        part[...] = total
        sum_rows(1)
        gram = full[1]
        yt = fdot(fdot(xwt, gram), gram)
        ut = fdot(whiten(yt), yt)
        left_gram(ut.T)
        sum_rows(2)

        pair_copy(lower_ref, lower_ref, 1).wait_recv()
        low = lower_ref[...]
        vt = fdot_nt(wt, low)
        pt = fdot(fdot(fdot(vt, full[2]), full[0]), full[2])
        yt = fdot(pt, low)
        kinv = whiten(yt)
        zt_ref[...] = fdot(kinv, pt)
        z_pair = pair_copy(zt_ref, zt_ref, 2)
        z_pair.start()
        ut = fdot(kinv, yt)
        bases_buf[...] = ut.T * bases_scale
        out_copies[1].start()
        ft = fdot_nt(ut, low)
        cuts = [(2, sent), (2 + sent, early)]
        for side in (0, 1):
            shape_cores(ft, side, 0, mh)
            for copy in ring_copies(side, 0, cuts):
                copy.start()
        out_copies[0].start()
        for k in range(1, half + 1):
            if k == max(half - 2, 1):
                pl.semaphore_wait(turn, 1)
            ring_step(k, cuts)

        def env(side, k):
            return ein[down_at(k) if side == 0 else up_at(k)]

        margin_pair(0).wait_recv()
        for k in range(half - 1, -1, -1):
            margin_work(k, env)
        swap_done()
        margin_scatter(0)
        margin_pair(1).wait_recv()
        margin_work(half, env)
        margin_scatter(1)
        margin_gather(0)
        margin_gather(1)
        margin_gathered(0)
        margins_out(0)
        margin_gathered(1)
        margins_out(1)
        out_copies[2].start()
        ring_sent(cuts)
        to_pair.wait_send()
        z_pair.wait_send()
        for copy in out_copies:
            copy.wait()


def deliver(*refs):
    sources, targets, buffers = refs[:3], refs[3:6], refs[6:9]
    into, out = refs[9:]
    spans = [
        (n, pl.ds(t * (src.shape[0] // count), src.shape[0] // count))
        for n, (src, count) in enumerate(zip(sources, (4, 1, 2)))
        for t in range(count)
    ]
    loads = [
        pltpu.make_async_copy(sources[n].at[span], buffers[n].at[span], into.at[t])
        for t, (n, span) in enumerate(spans)
    ]
    stores = [
        pltpu.make_async_copy(buffers[n].at[span], targets[n].at[span], out.at[t])
        for t, (n, span) in enumerate(spans)
    ]
    for copy in loads:
        copy.start()
    for load, store in zip(loads, stores):
        load.wait()
        store.start()
    for store in stores:
        store.wait()


def build(mesh):
    rows_n = mesh.shape["row"]
    vecs = mesh.shape["vec"]

    def local(train_cores, sketch, exit_sketch):
        _, rank, modes, _ = train_cores.shape
        kept = sketch.shape[1]
        half = vecs // 2
        mh = modes // 2
        early = EARLY if mh > EARLY else mh // 2
        ch = rank // rows_n
        ech = kept // rows_n
        dma = pltpu.SemaphoreType.DMA
        vmem = pl.BlockSpec(memory_space=pltpu.VMEM)
        shapes = (
            jax.ShapeDtypeStruct((kept * modes, kept), F32),
            jax.ShapeDtypeStruct((rank, kept), F32),
            jax.ShapeDtypeStruct((kept, vecs * kept), F32),
        )
        hbm = pl.BlockSpec(memory_space=pl.ANY)
        results = pl.pallas_call(
            functools.partial(kernel, (rank, kept, modes, rows_n, vecs)),
            out_shape=shapes,
            in_specs=[hbm, vmem, vmem],
            out_specs=(hbm, hbm, hbm),
            scratch_shapes=[
                pltpu.VMEM((rank // 128, rank * modes, 128), F32),
                pltpu.VMEM((modes * rank, rank), BF16),
                pltpu.VMEM((modes * rank, rank), BF16),
                pltpu.VMEM((modes * rank, rank), BF16),
                pltpu.VMEM((modes * rank, rank), BF16),
                pltpu.VMEM((rank, rank), F32),
                pltpu.VMEM((3, rows_n, ch, rank), F32),
                pltpu.VMEM((3, rank, rank), F32),
                pltpu.VMEM((rank, rank), F32),
                pltpu.VMEM((kept, rank), F32),
                pltpu.VMEM((kept, kept), F32),
                pltpu.VMEM((modes * rank, 2 * kept), BF16),
                pltpu.VMEM((modes * 2 * kept, 2 * kept), BF16),
                pltpu.VMEM((2, half + 1, (mh + 2) * kept, kept), F32),
                pltpu.VMEM((vecs, kept, kept), F32),
                pltpu.VMEM((rows_n, vecs, ech, kept), F32),
                pltpu.VMEM((half - 1, 2, kept, kept), F32),
                pltpu.VMEM((half - 1, 2, kept, kept), F32),
                pltpu.VMEM((vecs, kept, kept), F32),
                pltpu.VMEM((vecs, kept, kept), F32),
                pltpu.VMEM((kept * modes, kept), F32),
                pltpu.VMEM((rank, kept), F32),
                pltpu.VMEM((kept, vecs * kept), F32),
                dma((8, rank // 128)),
                dma((3,)), dma((3,)), dma((3,)), dma((3,)),
                dma((5,)), dma((5,)),
                dma((2, half, 2)), dma((2, half, 2)),
                dma((2,)), dma((2,)), dma((half - 1,)), dma((half - 1,)), dma((2,)), dma((2,)),
                dma((3,)),
                pltpu.VMEM((2, half + 1, early * rank, rank), F32),
                pltpu.VMEM((2, half + 1, kept, rank), F32),
                pltpu.VMEM((2, early * kept, rank), BF16),
                pltpu.VMEM((2, early * kept, rank), BF16),
                dma((2, half)), dma((2, half)), dma((2, half)), dma((2, half)),
                pltpu.SemaphoreType.REGULAR,
            ],
            compiler_params=pltpu.CompilerParams(
                collective_id=0, has_side_effects=True, vmem_limit_bytes=58 * 1024 * 1024
            ),
        )(train_cores.reshape(rank * modes, rank), sketch, exit_sketch)
        rounded, bases, margins = pl.pallas_call(
            deliver,
            out_shape=shapes,
            in_specs=[hbm] * 3,
            out_specs=(hbm, hbm, hbm),
            scratch_shapes=[pltpu.VMEM(x.shape, F32) for x in shapes] + [dma((7,)), dma((7,))],
        )(*results)
        return (
            rounded.reshape(1, kept, modes, kept),
            bases[None],
            margins[None],
        )

    return local


def solution(mesh):
    return jax.shard_map(
        build(mesh),
        mesh=mesh,
        in_specs=(P("vec", "cores", "row", None), P("cores", None), P()),
        out_specs=(
            P("vec", "cores", "row", None),
            P("vec", "cores", None),
            P("vec", "cores", None),
        ),
        check_vma=False,
    )
```
